128 devices in a mesh: ctx: 16 (over x, z), ch: 8 (over y, core).
Axes of the slice: x: 4, y: 4, z: 4, core: 2. Of those that a mesh axis runs over, the one named last changes fastest.
Arguments:
- inner_gate: bfloat16 [8192, 2048], P('ctx', 'ch'), may hold values from -6 to 6
- outer_gate: bfloat16 [8192, 2048], P('ctx', 'ch'), may hold values from -6 to 6
- source_values: bfloat16 [8192, 2048], P('ctx', 'ch'), may hold values from -6 to 6
- filter_taps: float32 [8192, 2048], P('ctx', 'ch'), may hold values from -1.1 to 1.1, as said below
- skip_gain: float32 [2048], P('ch'), may hold values from -1 to 1
- output_weight: bfloat16 [2048, 2048], replicated, may hold values from -0.125 to 0.125
Outputs:
- projected: bfloat16 [8192, 2048], P('ctx', 'ch')
The draws below stay inside these ranges and needn't reach their ends.
Inputs may be any that keep to these rules, and one draw needn't show every extreme that they name: `filter_taps`: filter taps for lags 0 to 8191 of each channel.
All inputs are finite; a program needn't handle non-finite values.
Results may differ from the reference program's by a relative error of at most 0.0049.
Values may be sent and summed in bfloat16 or wider, within the bound.
A program may use at most 128 MiB of HBM per device.

```python
import math
import jax
import jax.numpy as jnp

FILTER_WIDTH = 2048
DO = 2048
BASE_COUNT = 8192


def draw_filter_taps(key, part):
    key = jax.random.fold_in(key, 11)
    derived_seeds = jax.random.split(key, 9)
    chosen = jax.random.uniform(derived_seeds[0], (FILTER_WIDTH,))
    slow_share = 0.5
    rough_part = jnp.clip(jax.random.normal(derived_seeds[1], (BASE_COUNT, FILTER_WIDTH)), -4.0, 4.0)
    length_float = float(BASE_COUNT)
    slow_rate = jnp.exp(jax.random.uniform(derived_seeds[2], (FILTER_WIDTH,), minval=math.log(0.1 / length_float), maxval=math.log(1.0 / length_float)))
    middle_rate = jnp.exp(jax.random.uniform(derived_seeds[3], (FILTER_WIDTH,), minval=math.log(1.0 / length_float), maxval=math.log(1.0 / 60.0)))
    fast_rate = jnp.exp(jax.random.uniform(derived_seeds[4], (FILTER_WIDTH,), minval=math.log(1.0 / 50.0), maxval=math.log(1.0 / 30.0)))
    decay_rate = jnp.where(chosen < slow_share, slow_rate, jnp.where(chosen < slow_share + 0.5 * (1.0 - slow_share), middle_rate, fast_rate))
    delay_ordinal = jnp.arange(BASE_COUNT, dtype=jnp.int32)
    fading_profile = jnp.exp(-decay_rate[None, :] * delay_ordinal.astype(jnp.float32)[:, None])
    for spike_number in range(2):
        spike_location = jax.random.randint(derived_seeds[5 + 2 * spike_number], (FILTER_WIDTH,), 1, BASE_COUNT)
        spike_kept = jax.random.uniform(derived_seeds[6 + 2 * spike_number], (FILTER_WIDTH,), minval=0.6, maxval=0.8)
        fading_profile = fading_profile * jnp.where(delay_ordinal[:, None] >= spike_location[None, :], spike_kept[None, :], 1.0)
    normaliser = jnp.sqrt(2.0 * decay_rate / (1.0 - jnp.exp(-2.0 * decay_rate * length_float)))
    return (rough_part * fading_profile * normaliser[None, :]).astype(jnp.float32)


def steps_of(stream_key, extent, cuts, smallest, largest):
    def one(axis_at, shards_of):
        steps = jax.random.uniform(jax.random.fold_in(jax.random.fold_in(stream_key, 6), axis_at), (shards_of,), jnp.float32, smallest / len(cuts), largest / len(cuts))
        return jnp.repeat(jnp.exp(steps), extent[axis_at] // shards_of).reshape((-1,) + (1,) * (len(extent) - axis_at - 1))

    loudness = one(*cuts[0])
    for cut in cuts[1:]:
        loudness = loudness * one(*cut)
    return loudness


def normal_values(own_key, extent, width, bound, shards=(), kind=jnp.bfloat16):
    array = width * jax.random.normal(own_key, extent, jnp.float32)
    if shards:
        array = array * steps_of(own_key, extent, shards, -0.22, 0.18)
    return jnp.clip(array, -bound, bound).astype(kind)


def setup_inputs(seed: int = 0) -> dict:
    key_of = jax.random.split(jax.random.key(seed), 7)
    inner_gate = normal_values(key_of[0], (BASE_COUNT, FILTER_WIDTH), 1.0, 6.0, ((0, 16), (1, 8)))
    outer_gate = normal_values(key_of[1], (BASE_COUNT, FILTER_WIDTH), 1.0, 6.0, ((0, 16), (1, 8)))
    source_values = normal_values(key_of[2], (BASE_COUNT, FILTER_WIDTH), 1.0, 6.0, ((0, 16), (1, 8)))
    filter_taps = draw_filter_taps(jax.random.fold_in(key_of[6], 71), 0)
    skip_gain = jnp.clip(jax.random.uniform(key_of[4], (FILTER_WIDTH,), jnp.float32, -1.0, 1.0) * steps_of(key_of[4], (FILTER_WIDTH,), ((0, 8),), -0.4, 0.0), -1.0, 1.0)
    output_weight = normal_values(key_of[5], (FILTER_WIDTH, DO), FILTER_WIDTH ** -0.5, 0.125)
    return {"inner_gate": inner_gate, "outer_gate": outer_gate, "source_values": source_values, "filter_taps": filter_taps, "skip_gain": skip_gain, "output_weight": output_weight}


def reference(inner_gate, outer_gate, source_values, filter_taps, skip_gain, output_weight):
    signal = inner_gate.astype(jnp.float32) * source_values.astype(jnp.float32)
    padded_length = 2 * BASE_COUNT
    signal_spectrum = jnp.fft.rfft(signal, n=padded_length, axis=0)
    taps_spectrum = jnp.fft.rfft(filter_taps, n=padded_length, axis=0)
    convolved = jnp.fft.irfft(signal_spectrum * taps_spectrum, n=padded_length, axis=0)[:BASE_COUNT]
    convolved = convolved.astype(signal.dtype)
    gated_rows = (outer_gate.astype(jnp.float32) * (convolved + skip_gain[None, :] * signal)).astype(jnp.bfloat16)
    return jnp.dot(gated_rows, output_weight, preferred_element_type=jnp.float32).astype(jnp.bfloat16)
```

```python
import functools

import jax
import jax.numpy as jnp
import ml_dtypes
import numpy as np
from jax import lax
from jax.experimental import pallas as pl
from jax.experimental.pallas import tpu as pltpu
from jax.sharding import PartitionSpec as P

MESH = pl.DeviceIdType.MESH
F32 = jnp.float32
BF16 = jnp.bfloat16

CTX = 16
SIDE = 4
TOK = 512
CH = 256
LANES = 128
CHUNKS = 2
GROUP = 8
PHASES = 16
PER = TOK // PHASES
ROWS = CTX * PER
LENGTH = ROWS * PHASES
FEATURES = 256
HALF = TOK // 2
BLOCK = 128


def split_table(table):
    high = table.astype(np.float32).astype(ml_dtypes.bfloat16)
    low = (table - high.astype(np.float64)).astype(np.float32).astype(ml_dtypes.bfloat16)
    return np.stack([high, low])


def tables():
    k_row = np.arange(ROWS) + 0.25
    rows = np.arange(ROWS)
    turn = 2.0 * np.pi * np.outer(k_row, rows) / ROWS
    row_forward = np.concatenate([np.cos(turn), -np.sin(turn)], axis=0)
    row_inverse = np.concatenate([np.cos(turn.T), -np.sin(turn.T)], axis=1)
    phase = np.repeat(np.arange(PHASES), GROUP)
    twist = 2.0 * np.pi * np.outer(k_row, phase) / LENGTH
    twiddle = np.stack([np.cos(twist), -np.sin(twist)]).astype(np.float32)
    untwiddle = (np.stack([np.cos(twist), np.sin(twist)]) / LENGTH).astype(np.float32)
    angle = 2.0 * np.pi * np.outer(np.arange(PHASES), np.arange(PHASES)) / PHASES
    cosine = np.kron(np.cos(angle), np.eye(GROUP))
    sine = np.kron(np.sin(angle), np.eye(GROUP))
    phase_forward = np.block([[cosine, -sine], [sine, cosine]])
    phase_inverse = np.block([[cosine, sine], [-sine, cosine]])
    return (
        split_table(row_forward),
        split_table(row_inverse),
        twiddle,
        untwiddle,
        split_table(phase_forward),
        split_table(phase_inverse),
    )


def swap_groups(parts, roll):
    parts = list(parts)
    lane = lax.broadcasted_iota(jnp.int32, parts[0].shape, 1)
    bit = PHASES // 2
    while bit:
        shift = bit * GROUP
        upper = (lane & shift) != 0
        for q in range(PHASES):
            if q & bit:
                continue
            first, second = parts[q], parts[q | bit]
            parts[q] = jnp.where(upper, roll(second, shift), first)
            parts[q | bit] = jnp.where(upper, second, roll(first, LANES - shift))
        bit //= 2
    return parts


def lane_roll(value, shift):
    return pltpu.roll(value, shift, 1)


def split(value):
    high = value.astype(BF16)
    return high, (value - high.astype(F32)).astype(BF16)


def dot(a, b):
    return jnp.dot(a, b, preferred_element_type=F32)


def dot3(value, table):
    high, low = split(value)
    return dot(high, table[0]) + dot(low, table[0]) + dot(high, table[1])


def kernel(
    inner, outer, source, taps, skip, weight, row_f, row_i, twid, untwid, ph_f, ph_i,
    out,
    v_inner, v_outer, v_source, v_taps, v_skip, v_weight, v_row_f, v_row_i, v_twid, v_untwid, v_ph_f, v_ph_i,
    signal, send, recv, spectrum, y_send, y_recv, y_full, gated, acc,
    load_sem, a_send, a_recv, b_send, b_recv, c_send, c_recv, s_send, s_recv,
):
    me = lax.axis_index("ctx")
    rank = lax.axis_index("ch")
    x_me, z_me = me // SIDE, me % SIDE
    y_me, core = rank // 2, rank % 2
    up = lax.rem(y_me + 1, SIDE) * 2 + core
    down = lax.rem(y_me + SIDE - 1, SIDE) * 2 + core
    sibling = y_me * 2 + (1 - core)

    def peer(k):
        return lax.rem(x_me + k // SIDE, SIDE) * SIDE + lax.rem(z_me + k % SIDE, SIDE)

    feature0 = pl.multiple_of(rank * FEATURES, FEATURES)
    loads = [
        pltpu.make_async_copy(src, dst, load_sem.at[n])
        for n, (src, dst) in enumerate(
            [
                (inner, v_inner),
                (source, v_source),
                (taps.at[:, :LANES], v_taps.at[0]),
                (taps.at[:, LANES:], v_taps.at[1]),
                (row_f, v_row_f),
                (twid, v_twid),
                (ph_f, v_ph_f),
                (ph_i, v_ph_i),
                (untwid, v_untwid),
                (row_i, v_row_i),
                (outer, v_outer),
                (skip, v_skip),
                (weight.at[:, pl.ds(feature0, FEATURES)], v_weight),
            ]
        )
    ]
    for load in loads:
        load.start()

    barrier = pltpu.get_barrier_semaphore()
    for k in range(1, CTX):
        pl.semaphore_signal(barrier, inc=1, device_id=(peer(k), rank), device_id_type=MESH)
    for other in (up, down, sibling):
        pl.semaphore_signal(barrier, inc=1, device_id=(me, other), device_id_type=MESH)

    for load in loads[:4]:
        load.wait()
    for chunk in range(CHUNKS):
        lanes = slice(chunk * LANES, (chunk + 1) * LANES)
        signal[chunk] = v_inner[:, lanes].astype(F32) * v_source[:, lanes].astype(F32)

    far_first = sorted(range(1, CTX), key=lambda k: -(2 - abs(2 - k // SIDE)) - (2 - abs(2 - k % SIDE)))

    def a_copy(chunk, k):
        to = peer(k)
        return pltpu.make_async_remote_copy(
            src_ref=send.at[chunk, to],
            dst_ref=recv.at[chunk, me],
            send_sem=a_send.at[chunk, k],
            recv_sem=a_recv.at[chunk, k],
            device_id=(to, rank),
            device_id_type=MESH,
        )

    for chunk in range(CHUNKS):
        for place, ref in enumerate((signal, v_taps)):
            parts = swap_groups([ref[chunk, pl.ds(q, PER, stride=PHASES), :] for q in range(PHASES)], lane_roll)
            for d in range(CTX):
                send[chunk, d, :, place * LANES : (place + 1) * LANES] = parts[d].astype(BF16)
        if chunk == 0:
            pl.semaphore_wait(barrier, CTX + 2)
        for k in far_first:
            a_copy(chunk, k).start()
        recv[chunk, me] = send[chunk, me]

    def b_copy(chunk, k):
        to = peer(k)
        return pltpu.make_async_remote_copy(
            src_ref=y_send.at[chunk, pl.ds(pl.multiple_of(to * PER, PER), PER)],
            dst_ref=y_recv.at[chunk, me],
            send_sem=b_send.at[chunk, k],
            recv_sem=b_recv.at[chunk, k],
            device_id=(to, rank),
            device_id_type=MESH,
        )

    def convolve(chunk):
        for k in range(1, CTX):
            a_copy(chunk, k).wait_recv()
        if chunk == 0:
            for load in loads[4:10]:
                load.wait()
        arrived = recv[chunk].reshape(ROWS, 2 * LANES)
        for start in range(0, ROWS, BLOCK):
            real_rows = pl.ds(start, BLOCK)
            imag_rows = pl.ds(ROWS + start, BLOCK)
            real = dot(v_row_f[0, real_rows], arrived) + dot(v_row_f[1, real_rows], arrived)
            imag = dot(v_row_f[0, imag_rows], arrived) + dot(v_row_f[1, imag_rows], arrived)
            cosine, sine = v_twid[0, real_rows], v_twid[1, real_rows]
            turned = []
            for place in (0, 1):
                re = real[:, place * LANES : (place + 1) * LANES]
                im = imag[:, place * LANES : (place + 1) * LANES]
                turned.append(jnp.concatenate([re * cosine - im * sine, re * sine + im * cosine], axis=1))
            both = dot3(jnp.concatenate(turned, axis=0), v_ph_f)
            xr, xi = both[:BLOCK, :LANES], both[:BLOCK, LANES:]
            hr, hi = both[BLOCK:, :LANES], both[BLOCK:, LANES:]
            product = jnp.concatenate([xr * hr - xi * hi, xr * hi + xi * hr], axis=1)
            back = dot3(product, v_ph_i)
            re, im = back[:, :LANES], back[:, LANES:]
            cosine, sine = v_untwid[0, real_rows], v_untwid[1, real_rows]
            for rows, value in (
                (real_rows, re * cosine - im * sine),
                (imag_rows, re * sine + im * cosine),
            ):
                high, low = split(value)
                spectrum[rows, :LANES] = high
                spectrum[rows, LANES:] = low
        for dx in (2, 1, 3, 0):
            to_x = lax.rem(x_me + dx, SIDE)
            rows = pl.ds(pl.multiple_of(to_x * BLOCK, BLOCK), BLOCK)
            wide = dot(v_row_i[0, rows], spectrum[...])
            y = wide[:, :LANES] + wide[:, LANES:] + dot(v_row_i[1, rows], spectrum[:, :LANES])
            y_send[chunk, rows] = y.astype(BF16)
            for dz in (2, 1, 3, 0):
                if dx or dz:
                    b_copy(chunk, dx * SIDE + dz).start()
        y_recv[chunk, me] = y_send[chunk, pl.ds(pl.multiple_of(me * PER, PER), PER)]

    def half(ref, h):
        return ref.at[pl.ds(h * HALF, HALF)]

    def ring_copy(chunk, frm, to_slot, h, device, sem):
        return pltpu.make_async_remote_copy(
            src_ref=half(gated.at[frm, 0, chunk], h),
            dst_ref=half(gated.at[to_slot, 0, chunk], h),
            send_sem=c_send.at[chunk, sem],
            recv_sem=c_recv.at[chunk, sem],
            device_id=(me, device),
            device_id_type=MESH,
        )

    def ring(chunk, name, h):
        if name == "up":
            return ring_copy(chunk, 0, 1, h, up, h)
        if name == "down":
            return ring_copy(chunk, 0, 3, h, down, 2 + h)
        return ring_copy(chunk, 1 if h == 0 else 3, 2, h, up if h == 0 else down, 4 + h)

    def pair_copy(chunk, slot, h):
        return pltpu.make_async_remote_copy(
            src_ref=half(gated.at[slot, 0, chunk], h),
            dst_ref=half(gated.at[slot, 1, chunk], h),
            send_sem=s_send.at[chunk, slot, h],
            recv_sem=s_recv.at[chunk, slot, h],
            device_id=(me, sibling),
            device_id_type=MESH,
        )

    def gate(chunk):
        for k in range(1, CTX):
            b_copy(chunk, k).wait_recv()
        if chunk == 0:
            for load in loads[10:]:
                load.wait()
        lanes = slice(chunk * LANES, (chunk + 1) * LANES)
        parts = swap_groups([y_recv[chunk, d].astype(F32) for d in range(CTX)], lane_roll)
        for q in range(PHASES):
            y_full[pl.ds(q, PER, stride=PHASES), :] = parts[q]
        for h in (0, 1):
            rows = slice(h * HALF, (h + 1) * HALF)
            total = y_full[rows, :] + v_skip[0:1, lanes] * signal[chunk, rows]
            gated[0, 0, chunk, rows] = (v_outer[rows, lanes].astype(F32) * total).astype(BF16)
            ring(chunk, "up", h).start()
            ring(chunk, "down", h).start()
            pair_copy(chunk, 0, h).start()

    def project(chunk, slot, h, first=False, last=False):
        y_from = lax.rem(y_me + SIDE - slot, SIDE)
        rows = slice(h * HALF, (h + 1) * HALF)
        left = jnp.concatenate([gated[slot, 0, chunk, rows], gated[slot, 1, chunk, rows]], axis=1)
        right = jnp.concatenate(
            [
                v_weight[pl.ds(pl.multiple_of((2 * y_from + c) * CH + chunk * LANES, LANES), LANES), :]
                for c in (core, 1 - core)
            ],
            axis=0,
        )
        term = dot(left, right)
        if not first:
            term = acc[rows] + term
        if last:
            out[rows] = term.astype(BF16)
        else:
            acc[rows] = term

    def near(chunk):
        for name, slot, h, far in (("up", 1, 0, True), ("down", 3, 1, True), ("up", 1, 1, False), ("down", 3, 0, False)):
            ring(chunk, name, h).wait_recv()
            if far:
                ring(chunk, "far", h).start()
            pair_copy(chunk, slot, h).start()

    def own(chunk):
        for h in (0, 1):
            pair_copy(chunk, 0, h).wait_recv()
            project(chunk, 0, h, first=chunk == 0)

    def finish(chunk):
        for slot, h in ((1, 0), (3, 1), (1, 1), (3, 0)):
            pair_copy(chunk, slot, h).wait_recv()
            project(chunk, slot, h)
        for h in (0, 1):
            ring(chunk, "far", h).wait_recv()
            pair_copy(chunk, 2, h).start()
        for h in (0, 1):
            pair_copy(chunk, 2, h).wait_recv()
            project(chunk, 2, h, last=chunk == CHUNKS - 1)

    convolve(0)
    convolve(1)
    gate(0)
    gate(1)
    near(0)
    own(0)
    near(1)
    own(1)
    finish(0)
    finish(1)

    for chunk in range(CHUNKS):
        for k in range(1, CTX):
            a_copy(chunk, k).wait_send()
            b_copy(chunk, k).wait_send()
        for name in ("up", "down", "far"):
            for h in (0, 1):
                ring(chunk, name, h).wait_send()
        for slot in range(SIDE):
            for h in (0, 1):
                pair_copy(chunk, slot, h).wait_send()


def on_device(inner_gate, outer_gate, source_values, filter_taps, skip_gain, output_weight):
    constants = [jnp.asarray(table) for table in tables()]
    operands = (inner_gate, outer_gate, source_values, filter_taps, skip_gain.reshape(1, CH), output_weight, *constants)
    vmem = pltpu.VMEM
    dma = pltpu.SemaphoreType.DMA
    return pl.pallas_call(
        kernel,
        out_shape=jax.ShapeDtypeStruct((TOK, FEATURES), BF16),
        in_specs=[pl.BlockSpec(memory_space=pl.ANY)] * len(operands),
        out_specs=pl.BlockSpec(memory_space=pltpu.VMEM),
        scratch_shapes=[
            vmem((TOK, CH), BF16),
            vmem((TOK, CH), BF16),
            vmem((TOK, CH), BF16),
            vmem((CHUNKS, TOK, LANES), F32),
            vmem((1, CH), F32),
            vmem((output_weight.shape[0], FEATURES), BF16),
            *[vmem(table.shape, table.dtype) for table in constants],
            vmem((CHUNKS, TOK, LANES), F32),
            vmem((CHUNKS, CTX, PER, 2 * LANES), BF16),
            vmem((CHUNKS, CTX, PER, 2 * LANES), BF16),
            vmem((2 * ROWS, 2 * LANES), BF16),
            vmem((CHUNKS, ROWS, LANES), BF16),
            vmem((CHUNKS, CTX, PER, LANES), BF16),
            vmem((TOK, LANES), F32),
            vmem((SIDE, 2, CHUNKS, TOK, LANES), BF16),
            vmem((TOK, FEATURES), F32),
            dma((13,)),
            dma((CHUNKS, CTX)),
            dma((CHUNKS, CTX)),
            dma((CHUNKS, CTX)),
            dma((CHUNKS, CTX)),
            dma((CHUNKS, 6)),
            dma((CHUNKS, 6)),
            dma((CHUNKS, SIDE, 2)),
            dma((CHUNKS, SIDE, 2)),
        ],
        compiler_params=pltpu.CompilerParams(
            collective_id=0, has_side_effects=True, vmem_limit_bytes=48 * 1024 * 1024
        ),
        cost_estimate=pl.CostEstimate(flops=3 * 10**9, bytes_accessed=8 * 10**6, transcendentals=0),
        name="hyena",
    )(*operands)


def solution(mesh):
    in_specs = (P("ctx", "ch"), P("ctx", "ch"), P("ctx", "ch"), P("ctx", "ch"), P("ch"), P())
    out_specs = P("ctx", "ch")
    return jax.shard_map(
        on_device, mesh=mesh, in_specs=in_specs, out_specs=out_specs, check_vma=False
    )
```

```python
import functools

import jax
import jax.numpy as jnp
import ml_dtypes
import numpy as np
from jax import lax
from jax.experimental import pallas as pl
from jax.experimental.pallas import tpu as pltpu
from jax.sharding import PartitionSpec as P

MESH = pl.DeviceIdType.MESH
F32 = jnp.float32
BF16 = jnp.bfloat16

CTX = 16
SIDE = 4
TOK = 512
CH = 256
LANES = 128
CHUNKS = 2
GROUP = 8
PHASES = 16
PER = TOK // PHASES
ROWS = CTX * PER
LENGTH = ROWS * PHASES
FEATURES = 256
HALF = TOK // 2
BLOCK = 128


def split_table(table):
    high = table.astype(np.float32).astype(ml_dtypes.bfloat16)
    low = (table - high.astype(np.float64)).astype(np.float32).astype(ml_dtypes.bfloat16)
    return np.stack([high, low])


def tables():
    k_row = np.arange(ROWS) + 0.25
    rows = np.arange(ROWS)
    turn = 2.0 * np.pi * np.outer(k_row, rows) / ROWS
    row_forward = np.concatenate([np.cos(turn), -np.sin(turn)], axis=0)
    row_inverse = np.concatenate([np.cos(turn.T), -np.sin(turn.T)], axis=1)
    phase = np.repeat(np.arange(PHASES), GROUP)
    twist = 2.0 * np.pi * np.outer(k_row, phase) / LENGTH
    twiddle = np.stack([np.cos(twist), -np.sin(twist)]).astype(np.float32)
    untwiddle = (np.stack([np.cos(twist), np.sin(twist)]) / LENGTH).astype(np.float32)
    angle = 2.0 * np.pi * np.outer(np.arange(PHASES), np.arange(PHASES)) / PHASES
    cosine = np.kron(np.cos(angle), np.eye(GROUP))
    sine = np.kron(np.sin(angle), np.eye(GROUP))
    phase_forward = np.block([[cosine, -sine], [sine, cosine]])
    phase_inverse = np.block([[cosine, sine], [-sine, cosine]])
    return (
        split_table(row_forward),
        split_table(row_inverse),
        twiddle,
        untwiddle,
        split_table(phase_forward),
        split_table(phase_inverse),
    )


def swap_groups(parts, roll):
    parts = list(parts)
    lane = lax.broadcasted_iota(jnp.int32, parts[0].shape, 1)
    bit = PHASES // 2
    while bit:
        shift = bit * GROUP
        upper = (lane & shift) != 0
        for q in range(PHASES):
            if q & bit:
                continue
            first, second = parts[q], parts[q | bit]
            parts[q] = jnp.where(upper, roll(second, shift), first)
            parts[q | bit] = jnp.where(upper, second, roll(first, LANES - shift))
        bit //= 2
    return parts


def lane_roll(value, shift):
    return pltpu.roll(value, shift, 1)


def split(value):
    high = value.astype(BF16)
    return high, (value - high.astype(F32)).astype(BF16)


def dot(a, b):
    return jnp.dot(a, b, preferred_element_type=F32)


def dot3(value, table):
    high, low = split(value)
    return dot(high, table[0]) + dot(low, table[0]) + dot(high, table[1])


def kernel(
    inner, outer, source, taps, skip, weight, row_f, row_i, twid, untwid, ph_f, ph_i,
    out,
    v_inner, v_outer, v_source, v_taps, v_skip, v_weight, v_row_f, v_row_i, v_twid, v_untwid, v_ph_f, v_ph_i,
    signal, send, recv, spectrum, y_send, y_recv, y_full, gated, acc,
    load_sem, a_send, a_recv, b_send, b_recv, c_send, c_recv, s_send, s_recv,
):
    me = lax.axis_index("ctx")
    rank = lax.axis_index("ch")
    x_me, z_me = me // SIDE, me % SIDE
    y_me, core = rank // 2, rank % 2
    up = lax.rem(y_me + 1, SIDE) * 2 + core
    down = lax.rem(y_me + SIDE - 1, SIDE) * 2 + core
    sibling = y_me * 2 + (1 - core)

    def peer(k):
        return lax.rem(x_me + k // SIDE, SIDE) * SIDE + lax.rem(z_me + k % SIDE, SIDE)

    feature0 = pl.multiple_of(rank * FEATURES, FEATURES)
    loads = [
        pltpu.make_async_copy(src, dst, load_sem.at[n])
        for n, (src, dst) in enumerate(
            [
                (inner, v_inner),
                (source, v_source),
                (taps.at[:, :LANES], v_taps.at[0]),
                (taps.at[:, LANES:], v_taps.at[1]),
                (row_f, v_row_f),
                (twid, v_twid),
                (ph_f, v_ph_f),
                (ph_i, v_ph_i),
                (untwid, v_untwid),
                (row_i, v_row_i),
                (outer, v_outer),
                (skip, v_skip),
                (weight.at[:, pl.ds(feature0, FEATURES)], v_weight),
            ]
        )
    ]
    for load in loads[:4]:
        load.start()

    barrier = pltpu.get_barrier_semaphore()
    for k in range(1, CTX):
        pl.semaphore_signal(barrier, inc=1, device_id=(peer(k), rank), device_id_type=MESH)
    for other in (up, down, sibling):
        pl.semaphore_signal(barrier, inc=1, device_id=(me, other), device_id_type=MESH)

    for load in loads[:4]:
        load.wait()
    for chunk in range(CHUNKS):
        lanes = slice(chunk * LANES, (chunk + 1) * LANES)
        signal[chunk] = v_inner[:, lanes].astype(F32) * v_source[:, lanes].astype(F32)

    far_first = sorted(range(1, CTX), key=lambda k: -(2 - abs(2 - k // SIDE)) - (2 - abs(2 - k % SIDE)))

    def a_copy(chunk, k):
        to = peer(k)
        return pltpu.make_async_remote_copy(
            src_ref=send.at[chunk, to],
            dst_ref=recv.at[chunk, me],
            send_sem=a_send.at[chunk, k],
            recv_sem=a_recv.at[chunk, k],
            device_id=(to, rank),
            device_id_type=MESH,
        )

    for chunk in range(CHUNKS):
        for place, ref in enumerate((signal, v_taps)):
            parts = swap_groups([ref[chunk, pl.ds(q, PER, stride=PHASES), :] for q in range(PHASES)], lane_roll)
            for d in range(CTX):
                send[chunk, d, :, place * LANES : (place + 1) * LANES] = parts[d].astype(BF16)
        if chunk == 0:
            pl.semaphore_wait(barrier, CTX + 2)
        for k in far_first:
            a_copy(chunk, k).start()
        recv[chunk, me] = send[chunk, me]
        if chunk == 0:
            for load in loads[4:]:
                load.start()

    def b_copy(chunk, k):
        to = peer(k)
        return pltpu.make_async_remote_copy(
            src_ref=y_send.at[chunk, pl.ds(pl.multiple_of(to * PER, PER), PER)],
            dst_ref=y_recv.at[chunk, me],
            send_sem=b_send.at[chunk, k],
            recv_sem=b_recv.at[chunk, k],
            device_id=(to, rank),
            device_id_type=MESH,
        )

    def convolve(chunk):
        for k in range(1, CTX):
            a_copy(chunk, k).wait_recv()
        if chunk == 0:
            for load in loads[4:10]:
                load.wait()
        arrived = recv[chunk].reshape(ROWS, 2 * LANES)
        for start in range(0, ROWS, BLOCK):
            real_rows = pl.ds(start, BLOCK)
            imag_rows = pl.ds(ROWS + start, BLOCK)
            real = dot(v_row_f[0, real_rows], arrived) + dot(v_row_f[1, real_rows], arrived)
            imag = dot(v_row_f[0, imag_rows], arrived) + dot(v_row_f[1, imag_rows], arrived)
            cosine, sine = v_twid[0, real_rows], v_twid[1, real_rows]
            turned = []
            for place in (0, 1):
                re = real[:, place * LANES : (place + 1) * LANES]
                im = imag[:, place * LANES : (place + 1) * LANES]
                turned.append(jnp.concatenate([re * cosine - im * sine, re * sine + im * cosine], axis=1))
            both = dot3(jnp.concatenate(turned, axis=0), v_ph_f)
            xr, xi = both[:BLOCK, :LANES], both[:BLOCK, LANES:]
            hr, hi = both[BLOCK:, :LANES], both[BLOCK:, LANES:]
            product = jnp.concatenate([xr * hr - xi * hi, xr * hi + xi * hr], axis=1)
            back = dot3(product, v_ph_i)
            re, im = back[:, :LANES], back[:, LANES:]
            cosine, sine = v_untwid[0, real_rows], v_untwid[1, real_rows]
            for rows, value in (
                (real_rows, re * cosine - im * sine),
                (imag_rows, re * sine + im * cosine),
            ):
                high, low = split(value)
                spectrum[rows, :LANES] = high
                spectrum[rows, LANES:] = low
        for dx in (2, 1, 3, 0):
            to_x = lax.rem(x_me + dx, SIDE)
            rows = pl.ds(pl.multiple_of(to_x * BLOCK, BLOCK), BLOCK)
            wide = dot(v_row_i[0, rows], spectrum[...])
            y = wide[:, :LANES] + wide[:, LANES:] + dot(v_row_i[1, rows], spectrum[:, :LANES])
            y_send[chunk, rows] = y.astype(BF16)
            for dz in (2, 1, 3, 0):
                if dx or dz:
                    b_copy(chunk, dx * SIDE + dz).start()
        y_recv[chunk, me] = y_send[chunk, pl.ds(pl.multiple_of(me * PER, PER), PER)]

    def half(ref, h):
        return ref.at[pl.ds(h * HALF, HALF)]

    def ring_copy(chunk, frm, to_slot, h, device, sem):
        return pltpu.make_async_remote_copy(
            src_ref=half(gated.at[frm, 0, chunk], h),
            dst_ref=half(gated.at[to_slot, 0, chunk], h),
            send_sem=c_send.at[chunk, sem],
            recv_sem=c_recv.at[chunk, sem],
            device_id=(me, device),
            device_id_type=MESH,
        )

    def ring(chunk, name, h):
        if name == "up":
            return ring_copy(chunk, 0, 1, h, up, h)
        if name == "down":
            return ring_copy(chunk, 0, 3, h, down, 2 + h)
        return ring_copy(chunk, 1 if h == 0 else 3, 2, h, up if h == 0 else down, 4 + h)

    def pair_copy(chunk, slot, h):
        return pltpu.make_async_remote_copy(
            src_ref=half(gated.at[slot, 0, chunk], h),
            dst_ref=half(gated.at[slot, 1, chunk], h),
            send_sem=s_send.at[chunk, slot, h],
            recv_sem=s_recv.at[chunk, slot, h],
            device_id=(me, sibling),
            device_id_type=MESH,
        )

    def gate(chunk):
        for k in range(1, CTX):
            b_copy(chunk, k).wait_recv()
        if chunk == 0:
            for load in loads[10:]:
                load.wait()
        lanes = slice(chunk * LANES, (chunk + 1) * LANES)
        parts = swap_groups([y_recv[chunk, d].astype(F32) for d in range(CTX)], lane_roll)
        for q in range(PHASES):
            y_full[pl.ds(q, PER, stride=PHASES), :] = parts[q]
        for h in (0, 1):
            rows = slice(h * HALF, (h + 1) * HALF)
            total = y_full[rows, :] + v_skip[0:1, lanes] * signal[chunk, rows]
            gated[0, 0, chunk, rows] = (v_outer[rows, lanes].astype(F32) * total).astype(BF16)
            ring(chunk, "up", h).start()
            ring(chunk, "down", h).start()
            pair_copy(chunk, 0, h).start()

    def project(chunk, slot, h, first=False, last=False):
        y_from = lax.rem(y_me + SIDE - slot, SIDE)
        rows = slice(h * HALF, (h + 1) * HALF)
        left = jnp.concatenate([gated[slot, 0, chunk, rows], gated[slot, 1, chunk, rows]], axis=1)
        right = jnp.concatenate(
            [
                v_weight[pl.ds(pl.multiple_of((2 * y_from + c) * CH + chunk * LANES, LANES), LANES), :]
                for c in (core, 1 - core)
            ],
            axis=0,
        )
        term = dot(left, right)
        if not first:
            term = acc[rows] + term
        if last:
            out[rows] = term.astype(BF16)
        else:
            acc[rows] = term

    def near(chunk):
        for name, slot, h, far in (("up", 1, 0, True), ("down", 3, 1, True), ("up", 1, 1, False), ("down", 3, 0, False)):
            ring(chunk, name, h).wait_recv()
            if far:
                ring(chunk, "far", h).start()
            pair_copy(chunk, slot, h).start()

    def own(chunk):
        for h in (0, 1):
            pair_copy(chunk, 0, h).wait_recv()
            project(chunk, 0, h, first=chunk == 0)

    def finish(chunk):
        for slot, h in ((1, 0), (3, 1), (1, 1), (3, 0)):
            pair_copy(chunk, slot, h).wait_recv()
            project(chunk, slot, h)
        for h in (0, 1):
            ring(chunk, "far", h).wait_recv()
            pair_copy(chunk, 2, h).start()
        for h in (0, 1):
            pair_copy(chunk, 2, h).wait_recv()
            project(chunk, 2, h, last=chunk == CHUNKS - 1)

    convolve(0)
    convolve(1)
    gate(0)
    gate(1)
    near(0)
    own(0)
    near(1)
    own(1)
    finish(0)
    finish(1)

    for chunk in range(CHUNKS):
        for k in range(1, CTX):
            a_copy(chunk, k).wait_send()
            b_copy(chunk, k).wait_send()
        for name in ("up", "down", "far"):
            for h in (0, 1):
                ring(chunk, name, h).wait_send()
        for slot in range(SIDE):
            for h in (0, 1):
                pair_copy(chunk, slot, h).wait_send()


def on_device(inner_gate, outer_gate, source_values, filter_taps, skip_gain, output_weight):
    constants = [jnp.asarray(table) for table in tables()]
    operands = (inner_gate, outer_gate, source_values, filter_taps, skip_gain.reshape(1, CH), output_weight, *constants)
    vmem = pltpu.VMEM
    dma = pltpu.SemaphoreType.DMA
    return pl.pallas_call(
        kernel,
        out_shape=jax.ShapeDtypeStruct((TOK, FEATURES), BF16),
        in_specs=[pl.BlockSpec(memory_space=pltpu.HBM)] * len(operands),
        out_specs=pl.BlockSpec(memory_space=pltpu.VMEM),
        scratch_shapes=[
            vmem((TOK, CH), BF16),
            vmem((TOK, CH), BF16),
            vmem((TOK, CH), BF16),
            vmem((CHUNKS, TOK, LANES), F32),
            vmem((1, CH), F32),
            vmem((output_weight.shape[0], FEATURES), BF16),
            *[vmem(table.shape, table.dtype) for table in constants],
            vmem((CHUNKS, TOK, LANES), F32),
            vmem((CHUNKS, CTX, PER, 2 * LANES), BF16),
            vmem((CHUNKS, CTX, PER, 2 * LANES), BF16),
            vmem((2 * ROWS, 2 * LANES), BF16),
            vmem((CHUNKS, ROWS, LANES), BF16),
            vmem((CHUNKS, CTX, PER, LANES), BF16),
            vmem((TOK, LANES), F32),
            vmem((SIDE, 2, CHUNKS, TOK, LANES), BF16),
            vmem((TOK, FEATURES), F32),
            dma((13,)),
            dma((CHUNKS, CTX)),
            dma((CHUNKS, CTX)),
            dma((CHUNKS, CTX)),
            dma((CHUNKS, CTX)),
            dma((CHUNKS, 6)),
            dma((CHUNKS, 6)),
            dma((CHUNKS, SIDE, 2)),
            dma((CHUNKS, SIDE, 2)),
        ],
        compiler_params=pltpu.CompilerParams(
            collective_id=0, has_side_effects=True, vmem_limit_bytes=48 * 1024 * 1024
        ),
        cost_estimate=pl.CostEstimate(flops=3 * 10**9, bytes_accessed=8 * 10**6, transcendentals=0),
        name="hyena",
    )(*[pltpu.with_memory_space_constraint(operand, pltpu.HBM) for operand in operands])


def solution(mesh):
    in_specs = (P("ctx", "ch"), P("ctx", "ch"), P("ctx", "ch"), P("ctx", "ch"), P("ch"), P())
    out_specs = P("ctx", "ch")
    return jax.shard_map(
        on_device, mesh=mesh, in_specs=in_specs, out_specs=out_specs, check_vma=False
    )
```

```python
import functools

import jax
import jax.numpy as jnp
import ml_dtypes
import numpy as np
from jax import lax
from jax.experimental import pallas as pl
from jax.experimental.pallas import tpu as pltpu
from jax.sharding import PartitionSpec as P

MESH = pl.DeviceIdType.MESH
F32 = jnp.float32
BF16 = jnp.bfloat16

CTX = 16
SIDE = 4
TOK = 512
CH = 256
LANES = 128
TILES = 2
SUBS = 4
GROUP = 4
PHASES = 32
PER = TOK // PHASES
ROWS = CTX * PER
LENGTH = ROWS * PHASES
FEATURES = 256
HALF = TOK // 2
PIECE = HALF // 2
BLOCK = 128


def split_table(table, axis):
    high = table.astype(np.float32).astype(ml_dtypes.bfloat16)
    low = (table - high.astype(np.float64)).astype(np.float32).astype(ml_dtypes.bfloat16)
    if axis == 1:
        return np.concatenate([high, low], axis=1)
    return np.concatenate([high, high, low], axis=0)


def tables():
    k_row = np.arange(ROWS) + 0.25
    rows = np.arange(ROWS)
    turn = 2.0 * np.pi * np.outer(k_row, rows) / ROWS
    row_forward = np.concatenate([np.cos(turn), -np.sin(turn)], axis=0)
    row_inverse = np.concatenate([np.cos(turn.T), -np.sin(turn.T)], axis=1)
    phase = np.repeat(np.arange(PHASES), GROUP)
    twist = 2.0 * np.pi * np.outer(k_row, phase) / LENGTH
    twiddle = np.stack([np.cos(twist), -np.sin(twist)]).astype(np.float32)
    untwiddle = (np.stack([np.cos(twist), np.sin(twist)]) / LENGTH).astype(np.float32)
    angle = 2.0 * np.pi * np.outer(np.arange(PHASES), np.arange(PHASES)) / PHASES
    cosine = np.kron(np.cos(angle), np.eye(GROUP))
    sine = np.kron(np.sin(angle), np.eye(GROUP))
    phase_forward = np.block([[cosine, -sine], [sine, cosine]])
    phase_inverse = np.block([[cosine, sine], [-sine, cosine]])
    return (
        split_table(row_forward, 1),
        split_table(row_inverse, 1),
        twiddle,
        untwiddle,
        split_table(phase_forward, 0),
        split_table(phase_inverse, 0),
    )


def lane_bit(shape, width):
    return (lax.broadcasted_iota(jnp.int32, shape, 1) & width) != 0


def swap_groups(parts, roll):
    parts = list(parts)
    bit = CTX // 2
    while bit:
        shift = bit * GROUP
        upper = lane_bit(parts[0].shape, shift)
        for j in range(CTX):
            if j & bit:
                continue
            first, second = parts[j], parts[j | bit]
            parts[j] = jnp.where(upper, roll(second, shift), first)
            parts[j | bit] = jnp.where(upper, second, roll(first, LANES - shift))
        bit //= 2
    return parts


def pack(rows_of, e, roll):
    parts = []
    for j in range(CTX):
        first, second = rows_of(j), rows_of(j + CTX)
        upper = lane_bit(first.shape, LANES // 2)
        if e == 0:
            parts.append(jnp.where(upper, roll(second, LANES // 2), first))
        else:
            parts.append(jnp.where(upper, second, roll(first, LANES // 2)))
    return swap_groups(parts, roll)


def halves(rows, e):
    blocks = rows.reshape(PER, 2, PHASES // 2, LANES)
    first, second = blocks[:, 0].reshape(HALF, LANES), blocks[:, 1].reshape(HALF, LANES)
    upper = lane_bit(first.shape, LANES // 2)
    if e == 0:
        return jnp.where(upper, pltpu.roll(second, LANES // 2, 1), first)
    return jnp.where(upper, second, pltpu.roll(first, LANES // 2, 1))


def lane_roll(value, shift):
    return pltpu.roll(value, shift, 1)


def split(value):
    high = value.astype(BF16)
    return high, (value - high.astype(F32)).astype(BF16)


def dot(a, b):
    return jnp.dot(a, b, preferred_element_type=F32)


def dot3(value, table):
    high, low = split(value)
    return dot(jnp.concatenate([high, low, high], axis=1), table[...])


def kernel(
    inner, outer, source, taps, skip, weight, row_f, row_i, twid, untwid, ph_f, ph_i,
    out,
    v_inner, v_outer, v_source, v_taps, v_skip, v_weight, v_row_f, v_row_i, v_twid, v_untwid, v_ph_f, v_ph_i,
    signal, send, recv, y_send, y_recv, y_full, gates, skipped, gated, acc,
    load_sem, a_send, a_recv, b_send, b_recv, c_send, c_recv, s_send, s_recv,
):
    me = lax.axis_index("ctx")
    rank = lax.axis_index("ch")
    x_me, z_me = me // SIDE, me % SIDE
    y_me, core = rank // 2, rank % 2
    up = lax.rem(y_me + 1, SIDE) * 2 + core
    down = lax.rem(y_me + SIDE - 1, SIDE) * 2 + core
    sibling = y_me * 2 + (1 - core)

    def peer(k):
        return lax.rem(x_me + k // SIDE, SIDE) * SIDE + lax.rem(z_me + k % SIDE, SIDE)

    feature0 = pl.multiple_of(rank * FEATURES, FEATURES)
    pairs = []
    for tile in range(TILES):
        lanes = pl.ds(tile * LANES, LANES)
        pairs += [(src.at[:, lanes], dst.at[tile]) for src, dst in ((taps, v_taps), (inner, v_inner), (source, v_source))]
    pairs += [(row_f, v_row_f), (twid, v_twid), (ph_f, v_ph_f), (ph_i, v_ph_i), (untwid, v_untwid), (row_i, v_row_i)]
    pairs += [(outer, v_outer), (skip, v_skip), (weight.at[:, pl.ds(feature0, FEATURES)], v_weight)]
    loads = [pltpu.make_async_copy(src, dst, load_sem.at[n]) for n, (src, dst) in enumerate(pairs)]
    for load in loads[:6]:
        load.start()

    barrier = pltpu.get_barrier_semaphore()
    for k in range(1, CTX):
        pl.semaphore_signal(barrier, inc=1, device_id=(peer(k), rank), device_id_type=MESH)
    for other in (up, down, sibling):
        pl.semaphore_signal(barrier, inc=1, device_id=(me, other), device_id_type=MESH)

    far_first = sorted(range(1, CTX), key=lambda k: -(2 - abs(2 - k // SIDE)) - (2 - abs(2 - k % SIDE)))

    def a_copy(chunk, k):
        to = peer(k)
        return pltpu.make_async_remote_copy(
            src_ref=send.at[chunk, to],
            dst_ref=recv.at[chunk, me],
            send_sem=a_send.at[chunk, k],
            recv_sem=a_recv.at[chunk, k],
            device_id=(to, rank),
            device_id_type=MESH,
        )

    for chunk in range(SUBS):
        tile, e = chunk // 2, chunk % 2
        if e == 0:
            for load in loads[3 * tile : 3 * tile + 3]:
                load.wait()
            signal[tile] = v_inner[tile].astype(F32) * v_source[tile].astype(F32)
        for place, ref in enumerate((signal, v_taps)):
            parts = pack(lambda q: ref[tile, pl.ds(q, PER, stride=PHASES), :], e, lane_roll)
            for d in range(CTX):
                send[chunk, d, :, place * LANES : (place + 1) * LANES] = parts[d].astype(BF16)
        if chunk == 0:
            pl.semaphore_wait(barrier, CTX + 2)
        for k in far_first:
            a_copy(chunk, k).start()
        recv[chunk, me] = send[chunk, me]
        if chunk == 1:
            for load in loads[6:]:
                load.start()

    def b_copy(chunk, k):
        to = peer(k)
        return pltpu.make_async_remote_copy(
            src_ref=y_send.at[chunk, to],
            dst_ref=y_recv.at[chunk, me],
            send_sem=b_send.at[chunk, k],
            recv_sem=b_recv.at[chunk, k],
            device_id=(to, rank),
            device_id_type=MESH,
        )

    def convolve(chunk):
        for k in range(1, CTX):
            a_copy(chunk, k).wait_recv()
        if chunk == 0:
            for load in loads[6:12]:
                load.wait()
        arrived = recv[chunk].reshape(ROWS, 2 * LANES)
        arrived = jnp.concatenate([arrived, arrived], axis=0)
        starts = range(0, ROWS, BLOCK)
        staged = [
            (dot(v_row_f[start : start + BLOCK], arrived), dot(v_row_f[ROWS + start : ROWS + start + BLOCK], arrived))
            for start in starts
        ]
        spectra = []
        for start, (real, imag) in zip(starts, staged):
            cosine, sine = v_twid[0, start : start + BLOCK], v_twid[1, start : start + BLOCK]
            turned = []
            for place in (0, 1):
                re = real[:, place * LANES : (place + 1) * LANES]
                im = imag[:, place * LANES : (place + 1) * LANES]
                turned.append(jnp.concatenate([re * cosine - im * sine, re * sine + im * cosine], axis=1))
            spectra.append(dot3(jnp.concatenate(turned, axis=0), v_ph_f))
        backs = []
        for both in spectra:
            xr, xi = both[:BLOCK, :LANES], both[:BLOCK, LANES:]
            hr, hi = both[BLOCK:, :LANES], both[BLOCK:, LANES:]
            backs.append(dot3(jnp.concatenate([xr * hr - xi * hi, xr * hi + xi * hr], axis=1), v_ph_i))
        reals, imags = [], []
        for start, back in zip(starts, backs):
            re, im = back[:, :LANES], back[:, LANES:]
            cosine, sine = v_untwid[0, start : start + BLOCK], v_untwid[1, start : start + BLOCK]
            reals.append(jnp.concatenate(split(re * cosine - im * sine), axis=1))
            imags.append(jnp.concatenate(split(re * sine + im * cosine), axis=1))
        spectrum = jnp.concatenate(reals + imags, axis=0)
        spectrum = jnp.concatenate([spectrum, spectrum], axis=0)
        side_rows = SIDE * PER
        for pair in ((2, 1), (3, 0)):
            to_x = [lax.rem(x_me + dx, SIDE) for dx in pair]
            left = [v_row_i[pl.ds(pl.multiple_of(x * side_rows, side_rows), side_rows), :] for x in to_x]
            wide = dot(jnp.concatenate(left, axis=0), spectrum)
            y = (wide[:, :LANES] + wide[:, LANES:]).astype(BF16)
            for n, dx in enumerate(pair):
                block = y[n * side_rows : (n + 1) * side_rows].reshape(SIDE, PER, LANES)
                y_send[chunk, pl.ds(to_x[n] * SIDE, SIDE)] = block
                for dz in (2, 1, 3, 0):
                    if dx or dz:
                        b_copy(chunk, dx * SIDE + dz).start()
        y_recv[chunk, me] = y_send[chunk, me]

    def piece(ref, p):
        return ref.at[pl.ds(p * PIECE, PIECE)]

    def ring(chunk, name, p):
        frm, slot, column, device, index = {
            "up": (0, 1, 0, up, 0),
            "down": (0, 3, 0, down, 1),
            "far": ((1, 3)[p], 2, 0, (up, down)[p], 2),
            "cross": ((1, 3)[p], 2, 1, (up, down)[p], 3),
        }[name]
        return pltpu.make_async_remote_copy(
            src_ref=piece(gated.at[frm, column, chunk], p),
            dst_ref=piece(gated.at[slot, column, chunk], p),
            send_sem=c_send.at[chunk, index, p],
            recv_sem=c_recv.at[chunk, index, p],
            device_id=(me, device),
            device_id_type=MESH,
        )

    def pair(chunk, slot, p, column=0):
        return pltpu.make_async_remote_copy(
            src_ref=piece(gated.at[slot, column, chunk], p),
            dst_ref=piece(gated.at[slot, 1 - column, chunk], p),
            send_sem=s_send.at[chunk, slot + 2 * column, p],
            recv_sem=s_recv.at[chunk, slot + 2 * column, p],
            device_id=(me, sibling),
            device_id_type=MESH,
        )

    first_core, second_core = core == 0, core == 1

    def prepare():
        for load in loads[12:14]:
            load.wait()
        for chunk in range(SUBS):
            tile, e = chunk // 2, chunk % 2
            lanes = slice(tile * LANES, (tile + 1) * LANES)
            gates[chunk] = halves(v_outer[:, lanes].astype(F32), e)
            skipped[chunk] = halves(v_skip[0:1, lanes] * signal[tile], e)

    def gate(chunk):
        for k in range(1, CTX):
            b_copy(chunk, k).wait_recv()
        parts = swap_groups([y_recv[chunk, d].astype(F32) for d in range(CTX)], lane_roll)
        for j in range(CTX):
            y_full[pl.ds(j, PER, stride=CTX), :] = parts[j]
        gated[0, 0, chunk] = (gates[chunk] * (y_full[...] + skipped[chunk])).astype(BF16)
        for p in (0, 1):
            ring(chunk, "up", p).start()
            ring(chunk, "down", 1 - p).start()
        for p in (0, 1):
            pair(chunk, 0, p).start()

    def near(chunk):
        for name, slot, p in (("up", 1, 0), ("down", 3, 1)):
            ring(chunk, name, p).wait_recv()
            pair(chunk, slot, p).start()

            @pl.when(second_core)
            def _(p=p):
                ring(chunk, "far", p).start()

        for name, slot, p in (("up", 1, 1), ("down", 3, 0)):
            ring(chunk, name, p).wait_recv()
            pair(chunk, slot, p).start()

    def cross(chunk):
        @pl.when(second_core)
        def _():
            for slot, p in ((1, 0), (3, 1)):
                pair(chunk, slot, p).wait_recv()
                ring(chunk, "cross", p).start()

    def far(chunk):
        @pl.when(second_core)
        def _():
            for column, name in enumerate(("far", "cross")):
                for p in (0, 1):
                    ring(chunk, name, p).wait_recv()
                    pair(chunk, 2, p, column).start()

    def arrived_pairs(chunk, slot):
        if slot == 0:
            for p in (0, 1):
                pair(chunk, 0, p).wait_recv()
        elif slot == 2:

            @pl.when(first_core)
            def _():
                for column in (0, 1):
                    for p in (0, 1):
                        pair(chunk, 2, p, column).wait_recv()

        else:
            ahead = 0 if slot == 1 else 1

            @pl.when(first_core)
            def _():
                pair(chunk, slot, ahead).wait_recv()

            pair(chunk, slot, 1 - ahead).wait_recv()

    def project(chunk, slot, first=False, last=False):
        arrived_pairs(chunk, slot)
        if chunk == 0 and slot == 0:
            loads[14].wait()
        y_from = lax.rem(y_me + SIDE - slot, SIDE)
        width = LANES // 2
        right = []
        for c in (core, 1 - core):
            start = pl.multiple_of((2 * y_from + c) * CH + chunk * width, width)
            right += [v_weight[pl.ds(start, width), :]] * 2
        left = jnp.concatenate([gated[slot, 0, chunk], gated[slot, 1, chunk]], axis=1)
        upper = lane_bit(left.shape, width)
        none = jnp.zeros_like(left)
        left = jnp.concatenate([jnp.where(upper, none, left), jnp.where(upper, left, none)], axis=0)
        term = dot(left, jnp.concatenate(right, axis=0))
        if not first:
            term = acc[...] + term
        if last:
            rows = term.astype(BF16).reshape(2, PER, PHASES // 2, FEATURES)
            for h in (0, 1):
                for r in range(PER):
                    start = r * PHASES + h * (PHASES // 2)
                    out[start : start + PHASES // 2] = rows[h, r]
        else:
            acc[...] = term

    prepare()
    for chunk in range(SUBS):
        convolve(chunk)
    for chunk in range(SUBS):
        gate(chunk)
    near(0)
    near(1)
    near(2)
    cross(0)
    project(0, 0, first=True)
    near(3)
    cross(1)
    project(1, 0)
    cross(2)
    far(0)
    project(2, 0)
    project(0, 1)
    project(0, 3)
    cross(3)
    far(1)
    project(3, 0)
    project(1, 1)
    project(1, 3)
    far(2)
    project(0, 2)
    project(2, 1)
    project(2, 3)
    far(3)
    project(1, 2)
    project(3, 1)
    project(3, 3)
    project(2, 2)
    project(3, 2, last=True)

    for chunk in range(SUBS):
        for k in range(1, CTX):
            a_copy(chunk, k).wait_send()
            b_copy(chunk, k).wait_send()
        for p in (0, 1):
            ring(chunk, "up", p).wait_send()
            ring(chunk, "down", p).wait_send()
            for slot in (0, 1, 3):
                pair(chunk, slot, p).wait_send()

    @pl.when(second_core)
    def _():
        for chunk in range(SUBS):
            for p in (0, 1):
                ring(chunk, "far", p).wait_send()
                ring(chunk, "cross", p).wait_send()
                for column in (0, 1):
                    pair(chunk, 2, p, column).wait_send()


def on_device(inner_gate, outer_gate, source_values, filter_taps, skip_gain, output_weight):
    constants = [jnp.asarray(table) for table in tables()]
    operands = (inner_gate, outer_gate, source_values, filter_taps, skip_gain.reshape(1, CH), output_weight, *constants)
    vmem = pltpu.VMEM
    dma = pltpu.SemaphoreType.DMA
    return pl.pallas_call(
        kernel,
        out_shape=jax.ShapeDtypeStruct((TOK, FEATURES), BF16),
        in_specs=[pl.BlockSpec(memory_space=pltpu.HBM)] * len(operands),
        out_specs=pl.BlockSpec(memory_space=pltpu.VMEM),
        scratch_shapes=[
            vmem((TILES, TOK, LANES), BF16),
            vmem((TOK, CH), BF16),
            vmem((TILES, TOK, LANES), BF16),
            vmem((TILES, TOK, LANES), F32),
            vmem((1, CH), F32),
            vmem((output_weight.shape[0], FEATURES), BF16),
            *[vmem(table.shape, table.dtype) for table in constants],
            vmem((TILES, TOK, LANES), F32),
            vmem((SUBS, CTX, PER, 2 * LANES), BF16),
            vmem((SUBS, CTX, PER, 2 * LANES), BF16),
            vmem((SUBS, CTX, PER, LANES), BF16),
            vmem((SUBS, CTX, PER, LANES), BF16),
            vmem((HALF, LANES), F32),
            vmem((SUBS, HALF, LANES), F32),
            vmem((SUBS, HALF, LANES), F32),
            vmem((SIDE, 2, SUBS, HALF, LANES), BF16),
            vmem((TOK, FEATURES), F32),
            dma((15,)),
            dma((SUBS, CTX)),
            dma((SUBS, CTX)),
            dma((SUBS, CTX)),
            dma((SUBS, CTX)),
            dma((SUBS, 4, 2)),
            dma((SUBS, 4, 2)),
            dma((SUBS, 5, 2)),
            dma((SUBS, 5, 2)),
        ],
        compiler_params=pltpu.CompilerParams(
            collective_id=0, has_side_effects=True, vmem_limit_bytes=48 * 1024 * 1024
        ),
        cost_estimate=pl.CostEstimate(flops=3 * 10**9, bytes_accessed=8 * 10**6, transcendentals=0),
        name="hyena",
    )(*[pltpu.with_memory_space_constraint(operand, pltpu.HBM) for operand in operands])


def solution(mesh):
    in_specs = (P("ctx", "ch"), P("ctx", "ch"), P("ctx", "ch"), P("ctx", "ch"), P("ch"), P())
    out_specs = P("ctx", "ch")
    return jax.shard_map(
        on_device, mesh=mesh, in_specs=in_specs, out_specs=out_specs, check_vma=False
    )
```

```python
import functools

import jax
import jax.numpy as jnp
import ml_dtypes
import numpy as np
from jax import lax
from jax.experimental import pallas as pl
from jax.experimental.pallas import tpu as pltpu
from jax.sharding import PartitionSpec as P

MESH = pl.DeviceIdType.MESH
F32 = jnp.float32
BF16 = jnp.bfloat16

CTX = 16
SIDE = 4
TOK = 512
CH = 256
LANES = 128
TILES = 2
SUBS = 4
GROUP = 4
PHASES = 32
PER = TOK // PHASES
ROWS = CTX * PER
LENGTH = ROWS * PHASES
FEATURES = 256
HALF = TOK // 2
PIECE = HALF // 2
BLOCK = 128


def split_table(table, axis):
    high = table.astype(np.float32).astype(ml_dtypes.bfloat16)
    low = (table - high.astype(np.float64)).astype(np.float32).astype(ml_dtypes.bfloat16)
    if axis == 1:
        return np.concatenate([high, low], axis=1)
    return np.concatenate([high, high, low], axis=0)


def tables():
    k_row = np.arange(ROWS) + 0.25
    rows = np.arange(ROWS)
    turn = 2.0 * np.pi * np.outer(k_row, rows) / ROWS
    row_forward = np.concatenate([np.cos(turn), -np.sin(turn)], axis=0)
    row_inverse = np.concatenate([np.cos(turn.T), -np.sin(turn.T)], axis=1)
    phase = np.repeat(np.arange(PHASES), GROUP)
    twist = 2.0 * np.pi * np.outer(k_row, phase) / LENGTH
    twiddle = np.stack([np.cos(twist), -np.sin(twist)]).astype(np.float32)
    untwiddle = (np.stack([np.cos(twist), np.sin(twist)]) / LENGTH).astype(np.float32)
    angle = 2.0 * np.pi * np.outer(np.arange(PHASES), np.arange(PHASES)) / PHASES
    cosine = np.kron(np.cos(angle), np.eye(GROUP))
    sine = np.kron(np.sin(angle), np.eye(GROUP))
    phase_forward = np.block([[cosine, -sine], [sine, cosine]])
    phase_inverse = np.block([[cosine, sine], [-sine, cosine]])
    return (
        split_table(row_forward, 1),
        split_table(row_inverse, 1),
        twiddle,
        untwiddle,
        split_table(phase_forward, 0),
        split_table(phase_inverse, 0),
    )


def lane_bit(shape, width):
    return (lax.broadcasted_iota(jnp.int32, shape, 1) & width) != 0


def swap_groups(parts, roll):
    parts = list(parts)
    bit = CTX // 2
    while bit:
        shift = bit * GROUP
        upper = lane_bit(parts[0].shape, shift)
        for j in range(CTX):
            if j & bit:
                continue
            first, second = parts[j], parts[j | bit]
            parts[j] = jnp.where(upper, roll(second, shift), first)
            parts[j | bit] = jnp.where(upper, second, roll(first, LANES - shift))
        bit //= 2
    return parts


def pack(rows_of, e, roll):
    parts = []
    for j in range(CTX):
        first, second = rows_of(j), rows_of(j + CTX)
        upper = lane_bit(first.shape, LANES // 2)
        if e == 0:
            parts.append(jnp.where(upper, roll(second, LANES // 2), first))
        else:
            parts.append(jnp.where(upper, second, roll(first, LANES // 2)))
    return swap_groups(parts, roll)


def halves(rows, e):
    blocks = rows.reshape(PER, 2, PHASES // 2, LANES)
    first, second = blocks[:, 0].reshape(HALF, LANES), blocks[:, 1].reshape(HALF, LANES)
    upper = lane_bit(first.shape, LANES // 2)
    if e == 0:
        return jnp.where(upper, pltpu.roll(second, LANES // 2, 1), first)
    return jnp.where(upper, second, pltpu.roll(first, LANES // 2, 1))


def lane_roll(value, shift):
    return pltpu.roll(value, shift, 1)


def split(value):
    high = value.astype(BF16)
    return high, (value - high.astype(F32)).astype(BF16)


def dot(a, b):
    return jnp.dot(a, b, preferred_element_type=F32)


def dot3(value, table):
    high, low = split(value)
    return dot(jnp.concatenate([high, low, high], axis=1), table[...])


def kernel(
    inner, outer, source, taps, skip, weight, row_f, row_i, twid, untwid, ph_f, ph_i,
    out,
    v_inner, v_outer, v_source, v_taps, v_skip, v_weight, v_row_f, v_row_i, v_twid, v_untwid, v_ph_f, v_ph_i,
    signal, send, recv, y_send, y_recv, y_full, gates, skipped, gated, acc,
    load_sem, a_send, a_recv, b_send, b_recv, c_send, c_recv, s_send, s_recv,
):
    me = lax.axis_index("ctx")
    rank = lax.axis_index("ch")
    x_me, z_me = me // SIDE, me % SIDE
    y_me, core = rank // 2, rank % 2
    up = lax.rem(y_me + 1, SIDE) * 2 + core
    down = lax.rem(y_me + SIDE - 1, SIDE) * 2 + core
    sibling = y_me * 2 + (1 - core)

    def peer(k):
        return lax.rem(x_me + k // SIDE, SIDE) * SIDE + lax.rem(z_me + k % SIDE, SIDE)

    feature0 = pl.multiple_of(rank * FEATURES, FEATURES)
    pairs = []
    for tile in range(TILES):
        lanes = pl.ds(tile * LANES, LANES)
        pairs += [(src.at[:, lanes], dst.at[tile]) for src, dst in ((taps, v_taps), (inner, v_inner), (source, v_source))]
    pairs += [(row_f, v_row_f), (twid, v_twid), (ph_f, v_ph_f), (ph_i, v_ph_i), (untwid, v_untwid), (row_i, v_row_i)]
    pairs += [(outer, v_outer), (skip, v_skip), (weight.at[:, pl.ds(feature0, FEATURES)], v_weight)]
    loads = [pltpu.make_async_copy(src, dst, load_sem.at[n]) for n, (src, dst) in enumerate(pairs)]
    for load in loads[:6]:
        load.start()

    barrier = pltpu.get_barrier_semaphore()
    for k in range(1, CTX):
        pl.semaphore_signal(barrier, inc=1, device_id=(peer(k), rank), device_id_type=MESH)
    for other in (up, down, sibling):
        pl.semaphore_signal(barrier, inc=1, device_id=(me, other), device_id_type=MESH)

    far_first = sorted(range(1, CTX), key=lambda k: -(2 - abs(2 - k // SIDE)) - (2 - abs(2 - k % SIDE)))

    def all_of(ref, chunk, send_sem, recv_sem):
        ref = ref.at[chunk, pl.ds(0, CTX - 1)]
        return pltpu.make_async_remote_copy(
            src_ref=ref,
            dst_ref=ref,
            send_sem=send_sem.at[chunk],
            recv_sem=recv_sem.at[chunk],
            device_id=(me, sibling),
            device_id_type=MESH,
        )

    def a_copy(chunk, k):
        to = peer(k)
        return pltpu.make_async_remote_copy(
            src_ref=send.at[chunk, to],
            dst_ref=recv.at[chunk, me],
            send_sem=a_send.at[chunk],
            recv_sem=a_recv.at[chunk],
            device_id=(to, rank),
            device_id_type=MESH,
        )

    for chunk in range(SUBS):
        tile, e = chunk // 2, chunk % 2
        if e == 0:
            for load in loads[3 * tile : 3 * tile + 3]:
                load.wait()
            signal[tile] = v_inner[tile].astype(F32) * v_source[tile].astype(F32)
        for place, ref in enumerate((signal, v_taps)):
            parts = pack(lambda q: ref[tile, pl.ds(q, PER, stride=PHASES), :], e, lane_roll)
            for d in range(CTX):
                send[chunk, d, :, place * LANES : (place + 1) * LANES] = parts[d].astype(BF16)
        if chunk == 0:
            pl.semaphore_wait(barrier, CTX + 2)
        for k in far_first:
            a_copy(chunk, k).start()
        recv[chunk, me] = send[chunk, me]
        if chunk == 1:
            for load in loads[6:]:
                load.start()

    def b_copy(chunk, k):
        to = peer(k)
        return pltpu.make_async_remote_copy(
            src_ref=y_send.at[chunk, to],
            dst_ref=y_recv.at[chunk, me],
            send_sem=b_send.at[chunk],
            recv_sem=b_recv.at[chunk],
            device_id=(to, rank),
            device_id_type=MESH,
        )

    def convolve(chunk):
        all_of(recv, chunk, a_send, a_recv).wait_recv()
        if chunk == 0:
            for load in loads[6:12]:
                load.wait()
        arrived = recv[chunk].reshape(ROWS, 2 * LANES)
        arrived = jnp.concatenate([arrived, arrived], axis=0)
        starts = range(0, ROWS, BLOCK)
        staged = [
            (dot(v_row_f[start : start + BLOCK], arrived), dot(v_row_f[ROWS + start : ROWS + start + BLOCK], arrived))
            for start in starts
        ]
        spectra = []
        for start, (real, imag) in zip(starts, staged):
            cosine, sine = v_twid[0, start : start + BLOCK], v_twid[1, start : start + BLOCK]
            turned = []
            for place in (0, 1):
                re = real[:, place * LANES : (place + 1) * LANES]
                im = imag[:, place * LANES : (place + 1) * LANES]
                turned.append(jnp.concatenate([re * cosine - im * sine, re * sine + im * cosine], axis=1))
            spectra.append(dot3(jnp.concatenate(turned, axis=0), v_ph_f))
        backs = []
        for both in spectra:
            xr, xi = both[:BLOCK, :LANES], both[:BLOCK, LANES:]
            hr, hi = both[BLOCK:, :LANES], both[BLOCK:, LANES:]
            backs.append(dot3(jnp.concatenate([xr * hr - xi * hi, xr * hi + xi * hr], axis=1), v_ph_i))
        reals, imags = [], []
        for start, back in zip(starts, backs):
            re, im = back[:, :LANES], back[:, LANES:]
            cosine, sine = v_untwid[0, start : start + BLOCK], v_untwid[1, start : start + BLOCK]
            reals.append(jnp.concatenate(split(re * cosine - im * sine), axis=1))
            imags.append(jnp.concatenate(split(re * sine + im * cosine), axis=1))
        spectrum = jnp.concatenate(reals + imags, axis=0)
        spectrum = jnp.concatenate([spectrum, spectrum], axis=0)
        side_rows = SIDE * PER
        for pair in ((2, 1), (3, 0)):
            to_x = [lax.rem(x_me + dx, SIDE) for dx in pair]
            left = [v_row_i[pl.ds(pl.multiple_of(x * side_rows, side_rows), side_rows), :] for x in to_x]
            wide = dot(jnp.concatenate(left, axis=0), spectrum)
            y = (wide[:, :LANES] + wide[:, LANES:]).astype(BF16)
            for n, dx in enumerate(pair):
                block = y[n * side_rows : (n + 1) * side_rows].reshape(SIDE, PER, LANES)
                y_send[chunk, pl.ds(to_x[n] * SIDE, SIDE)] = block
                for dz in (2, 1, 3, 0):
                    if dx or dz:
                        b_copy(chunk, dx * SIDE + dz).start()
        y_recv[chunk, me] = y_send[chunk, me]

    def piece(ref, p):
        return ref.at[pl.ds(p * PIECE, PIECE)]

    def ring(chunk, name, p):
        frm, slot, column, device, index = {
            "up": (0, 1, 0, up, 0),
            "down": (0, 3, 0, down, 1),
            "far": ((1, 3)[p], 2, 0, (up, down)[p], 2),
            "cross": ((1, 3)[p], 2, 1, (up, down)[p], 3),
        }[name]
        return pltpu.make_async_remote_copy(
            src_ref=piece(gated.at[frm, column, chunk], p),
            dst_ref=piece(gated.at[slot, column, chunk], p),
            send_sem=c_send.at[chunk, index, p],
            recv_sem=c_recv.at[chunk, index, p],
            device_id=(me, device),
            device_id_type=MESH,
        )

    def pair(chunk, slot, p, column=0):
        return pltpu.make_async_remote_copy(
            src_ref=piece(gated.at[slot, column, chunk], p),
            dst_ref=piece(gated.at[slot, 1 - column, chunk], p),
            send_sem=s_send.at[chunk, slot + 2 * column, p],
            recv_sem=s_recv.at[chunk, slot + 2 * column, p],
            device_id=(me, sibling),
            device_id_type=MESH,
        )

    first_core, second_core = core == 0, core == 1

    def prepare():
        for load in loads[12:14]:
            load.wait()
        for chunk in range(SUBS):
            tile, e = chunk // 2, chunk % 2
            lanes = slice(tile * LANES, (tile + 1) * LANES)
            gates[chunk] = halves(v_outer[:, lanes].astype(F32), e)
            skipped[chunk] = halves(v_skip[0:1, lanes] * signal[tile], e)

    def gate(chunk):
        all_of(y_recv, chunk, b_send, b_recv).wait_recv()
        parts = swap_groups([y_recv[chunk, d].astype(F32) for d in range(CTX)], lane_roll)
        for j in range(CTX):
            y_full[pl.ds(j, PER, stride=CTX), :] = parts[j]
        gated[0, 0, chunk] = (gates[chunk] * (y_full[...] + skipped[chunk])).astype(BF16)
        for p in (0, 1):
            ring(chunk, "up", p).start()
            ring(chunk, "down", 1 - p).start()
        for p in (0, 1):
            pair(chunk, 0, p).start()

    def near(chunk):
        for name, slot, p in (("up", 1, 0), ("down", 3, 1)):
            ring(chunk, name, p).wait_recv()
            pair(chunk, slot, p).start()

            @pl.when(second_core)
            def _(p=p):
                ring(chunk, "far", p).start()

        for name, slot, p in (("up", 1, 1), ("down", 3, 0)):
            ring(chunk, name, p).wait_recv()
            pair(chunk, slot, p).start()

    def cross(chunk):
        @pl.when(second_core)
        def _():
            for slot, p in ((1, 0), (3, 1)):
                pair(chunk, slot, p).wait_recv()
                ring(chunk, "cross", p).start()

    def far(chunk):
        @pl.when(second_core)
        def _():
            for column, name in enumerate(("far", "cross")):
                for p in (0, 1):
                    ring(chunk, name, p).wait_recv()
                    pair(chunk, 2, p, column).start()

    def arrived_pairs(chunk, slot):
        if slot == 0:
            for p in (0, 1):
                pair(chunk, 0, p).wait_recv()
        elif slot == 2:

            @pl.when(first_core)
            def _():
                for column in (0, 1):
                    for p in (0, 1):
                        pair(chunk, 2, p, column).wait_recv()

        else:
            ahead = 0 if slot == 1 else 1

            @pl.when(first_core)
            def _():
                pair(chunk, slot, ahead).wait_recv()

            pair(chunk, slot, 1 - ahead).wait_recv()

    def project(chunk, slot, first=False, last=False):
        arrived_pairs(chunk, slot)
        if chunk == 0 and slot == 0:
            loads[14].wait()
        y_from = lax.rem(y_me + SIDE - slot, SIDE)
        width = LANES // 2
        right = []
        for c in (core, 1 - core):
            start = pl.multiple_of((2 * y_from + c) * CH + chunk * width, width)
            right += [v_weight[pl.ds(start, width), :]] * 2
        left = jnp.concatenate([gated[slot, 0, chunk], gated[slot, 1, chunk]], axis=1)
        upper = lane_bit(left.shape, width)
        none = jnp.zeros_like(left)
        left = jnp.concatenate([jnp.where(upper, none, left), jnp.where(upper, left, none)], axis=0)
        term = dot(left, jnp.concatenate(right, axis=0))
        if not first:
            term = acc[...] + term
        if last:
            rows = term.astype(BF16).reshape(2, PER, PHASES // 2, FEATURES)
            for h in (0, 1):
                for r in range(PER):
                    start = r * PHASES + h * (PHASES // 2)
                    out[start : start + PHASES // 2] = rows[h, r]
        else:
            acc[...] = term

    prepare()
    for chunk in range(SUBS):
        convolve(chunk)
    for chunk in range(SUBS):
        gate(chunk)
    for chunk in range(SUBS):
        all_of(recv, chunk, a_send, a_recv).wait_send()
    near(0)
    for chunk in range(SUBS):
        all_of(y_recv, chunk, b_send, b_recv).wait_send()
    near(1)
    near(2)
    cross(0)
    project(0, 0, first=True)
    near(3)
    cross(1)
    project(1, 0)
    cross(2)
    far(0)
    project(2, 0)
    project(0, 1)
    project(0, 3)
    cross(3)
    far(1)
    project(3, 0)
    project(1, 1)
    project(1, 3)
    far(2)
    project(0, 2)
    project(2, 1)
    project(2, 3)
    far(3)
    project(1, 2)
    project(3, 1)
    project(3, 3)
    project(2, 2)
    project(3, 2, last=True)

    for chunk in range(SUBS):
        for p in (0, 1):
            ring(chunk, "up", p).wait_send()
            ring(chunk, "down", p).wait_send()
            for slot in (0, 1, 3):
                pair(chunk, slot, p).wait_send()

    @pl.when(second_core)
    def _():
        for chunk in range(SUBS):
            for p in (0, 1):
                ring(chunk, "far", p).wait_send()
                ring(chunk, "cross", p).wait_send()
                for column in (0, 1):
                    pair(chunk, 2, p, column).wait_send()


def on_device(inner_gate, outer_gate, source_values, filter_taps, skip_gain, output_weight):
    constants = [jnp.asarray(table) for table in tables()]
    operands = (inner_gate, outer_gate, source_values, filter_taps, skip_gain.reshape(1, CH), output_weight, *constants)
    vmem = pltpu.VMEM
    dma = pltpu.SemaphoreType.DMA
    return pl.pallas_call(
        kernel,
        out_shape=jax.ShapeDtypeStruct((TOK, FEATURES), BF16),
        in_specs=[pl.BlockSpec(memory_space=pltpu.HBM)] * len(operands),
        out_specs=pl.BlockSpec(memory_space=pltpu.VMEM),
        scratch_shapes=[
            vmem((TILES, TOK, LANES), BF16),
            vmem((TOK, CH), BF16),
            vmem((TILES, TOK, LANES), BF16),
            vmem((TILES, TOK, LANES), F32),
            vmem((1, CH), F32),
            vmem((output_weight.shape[0], FEATURES), BF16),
            *[vmem(table.shape, table.dtype) for table in constants],
            vmem((TILES, TOK, LANES), F32),
            vmem((SUBS, CTX, PER, 2 * LANES), BF16),
            vmem((SUBS, CTX, PER, 2 * LANES), BF16),
            vmem((SUBS, CTX, PER, LANES), BF16),
            vmem((SUBS, CTX, PER, LANES), BF16),
            vmem((HALF, LANES), F32),
            vmem((SUBS, HALF, LANES), F32),
            vmem((SUBS, HALF, LANES), F32),
            vmem((SIDE, 2, SUBS, HALF, LANES), BF16),
            vmem((TOK, FEATURES), F32),
            dma((15,)),
            dma((SUBS,)),
            dma((SUBS,)),
            dma((SUBS,)),
            dma((SUBS,)),
            dma((SUBS, 4, 2)),
            dma((SUBS, 4, 2)),
            dma((SUBS, 5, 2)),
            dma((SUBS, 5, 2)),
        ],
        compiler_params=pltpu.CompilerParams(
            collective_id=0, has_side_effects=True, vmem_limit_bytes=48 * 1024 * 1024
        ),
        cost_estimate=pl.CostEstimate(flops=3 * 10**9, bytes_accessed=8 * 10**6, transcendentals=0),
        name="hyena",
    )(*[pltpu.with_memory_space_constraint(operand, pltpu.HBM) for operand in operands])


def solution(mesh):
    in_specs = (P("ctx", "ch"), P("ctx", "ch"), P("ctx", "ch"), P("ctx", "ch"), P("ch"), P())
    out_specs = P("ctx", "ch")
    return jax.shard_map(
        on_device, mesh=mesh, in_specs=in_specs, out_specs=out_specs, check_vma=False
    )
```

```python
import functools

import jax
import jax.numpy as jnp
import ml_dtypes
import numpy as np
from jax import lax
from jax.experimental import pallas as pl
from jax.experimental.pallas import tpu as pltpu
from jax.sharding import PartitionSpec as P

MESH = pl.DeviceIdType.MESH
F32 = jnp.float32
BF16 = jnp.bfloat16

CTX = 16
SIDE = 4
TOK = 512
CH = 256
LANES = 128
TILES = 2
SUBS = 4
GROUP = 4
PHASES = 32
PER = TOK // PHASES
ROWS = CTX * PER
LENGTH = ROWS * PHASES
FEATURES = 256
HALF = TOK // 2
PIECE = HALF // 2
BLOCK = 128


def split_table(table, axis):
    high = table.astype(np.float32).astype(ml_dtypes.bfloat16)
    low = (table - high.astype(np.float64)).astype(np.float32).astype(ml_dtypes.bfloat16)
    if axis == 1:
        return np.concatenate([high, low], axis=1)
    return np.concatenate([high, high, low], axis=0)


def tables():
    k_row = np.arange(ROWS) + 0.25
    rows = np.arange(ROWS)
    turn = 2.0 * np.pi * np.outer(k_row, rows) / ROWS
    row_forward = np.concatenate([np.cos(turn), -np.sin(turn)], axis=0)
    row_inverse = np.concatenate([np.cos(turn.T), -np.sin(turn.T)], axis=1)
    phase = np.repeat(np.arange(PHASES), GROUP)
    twist = 2.0 * np.pi * np.outer(k_row, phase) / LENGTH
    twiddle = np.stack([np.cos(twist), -np.sin(twist)]).astype(np.float32)
    untwiddle = (np.stack([np.cos(twist), np.sin(twist)]) / LENGTH).astype(np.float32)
    angle = 2.0 * np.pi * np.outer(np.arange(PHASES), np.arange(PHASES)) / PHASES
    cosine = np.kron(np.cos(angle), np.eye(GROUP))
    sine = np.kron(np.sin(angle), np.eye(GROUP))
    phase_forward = np.block([[cosine, -sine], [sine, cosine]])
    phase_inverse = np.block([[cosine, sine], [-sine, cosine]])
    return (
        split_table(row_forward, 1),
        split_table(row_inverse, 1),
        twiddle,
        untwiddle,
        split_table(phase_forward, 0),
        split_table(phase_inverse, 0),
    )


def lane_bit(shape, width):
    return (lax.broadcasted_iota(jnp.int32, shape, 1) & width) != 0


def swap_groups(parts, roll):
    parts = list(parts)
    bit = CTX // 2
    while bit:
        shift = bit * GROUP
        upper = lane_bit(parts[0].shape, shift)
        for j in range(CTX):
            if j & bit:
                continue
            first, second = parts[j], parts[j | bit]
            parts[j] = jnp.where(upper, roll(second, shift), first)
            parts[j | bit] = jnp.where(upper, second, roll(first, LANES - shift))
        bit //= 2
    return parts


def pack(rows_of, e, roll):
    parts = []
    for j in range(CTX):
        first, second = rows_of(j), rows_of(j + CTX)
        upper = lane_bit(first.shape, LANES // 2)
        if e == 0:
            parts.append(jnp.where(upper, roll(second, LANES // 2), first))
        else:
            parts.append(jnp.where(upper, second, roll(first, LANES // 2)))
    return swap_groups(parts, roll)


def halves(rows, e):
    blocks = rows.reshape(PER, 2, PHASES // 2, LANES)
    first, second = blocks[:, 0].reshape(HALF, LANES), blocks[:, 1].reshape(HALF, LANES)
    upper = lane_bit(first.shape, LANES // 2)
    if e == 0:
        return jnp.where(upper, pltpu.roll(second, LANES // 2, 1), first)
    return jnp.where(upper, second, pltpu.roll(first, LANES // 2, 1))


def lane_roll(value, shift):
    return pltpu.roll(value, shift, 1)


def split(value):
    high = value.astype(BF16)
    return high, (value - high.astype(F32)).astype(BF16)


def dot(a, b):
    return jnp.dot(a, b, preferred_element_type=F32)


def dot3(value, table):
    high, low = split(value)
    return dot(jnp.concatenate([high, low, high], axis=1), table[...])


def kernel(
    inner, outer, source, taps, skip, weight, row_f, row_i, twid, untwid, ph_f, ph_i,
    out,
    v_inner, v_outer, v_source, v_taps, v_skip, v_weight, v_row_f, v_row_i, v_twid, v_untwid, v_ph_f, v_ph_i,
    signal, send, recv, y_send, y_recv, y_full, gates, skipped, gated, acc,
    load_sem, a_send, a_recv, b_send, b_recv, c_send, c_recv, s_send, s_recv,
):
    me = lax.axis_index("ctx")
    rank = lax.axis_index("ch")
    x_me, z_me = me // SIDE, me % SIDE
    y_me, core = rank // 2, rank % 2
    up = lax.rem(y_me + 1, SIDE) * 2 + core
    down = lax.rem(y_me + SIDE - 1, SIDE) * 2 + core
    sibling = y_me * 2 + (1 - core)

    def peer(k):
        return lax.rem(x_me + k // SIDE, SIDE) * SIDE + lax.rem(z_me + k % SIDE, SIDE)

    feature0 = pl.multiple_of(rank * FEATURES, FEATURES)
    pairs = []
    for tile in range(TILES):
        lanes = pl.ds(tile * LANES, LANES)
        pairs += [(src.at[:, lanes], dst.at[tile]) for src, dst in ((taps, v_taps), (inner, v_inner), (source, v_source))]
    pairs += [(row_f, v_row_f), (twid, v_twid), (ph_f, v_ph_f), (ph_i, v_ph_i), (untwid, v_untwid), (row_i, v_row_i)]
    pairs += [(outer, v_outer), (skip, v_skip), (weight.at[:, pl.ds(feature0, FEATURES)], v_weight)]
    loads = [pltpu.make_async_copy(src, dst, load_sem.at[n]) for n, (src, dst) in enumerate(pairs)]
    for load in loads[:6]:
        load.start()

    barrier = pltpu.get_barrier_semaphore()
    for k in range(1, CTX):
        pl.semaphore_signal(barrier, inc=1, device_id=(peer(k), rank), device_id_type=MESH)
    for other in (up, down, sibling):
        pl.semaphore_signal(barrier, inc=1, device_id=(me, other), device_id_type=MESH)

    far_first = sorted(range(1, CTX), key=lambda k: -(2 - abs(2 - k // SIDE)) - (2 - abs(2 - k % SIDE)))

    def all_of(ref, chunk, send_sem, recv_sem):
        ref = ref.at[chunk, pl.ds(0, CTX - 1)]
        return pltpu.make_async_remote_copy(
            src_ref=ref,
            dst_ref=ref,
            send_sem=send_sem.at[chunk],
            recv_sem=recv_sem.at[chunk],
            device_id=(me, sibling),
            device_id_type=MESH,
        )

    def a_copy(chunk, k):
        to = peer(k)
        return pltpu.make_async_remote_copy(
            src_ref=send.at[chunk, to],
            dst_ref=recv.at[chunk, me],
            send_sem=a_send.at[chunk],
            recv_sem=a_recv.at[chunk],
            device_id=(to, rank),
            device_id_type=MESH,
        )

    for chunk in range(SUBS):
        tile, e = chunk // 2, chunk % 2
        if e == 0:
            for load in loads[3 * tile : 3 * tile + 3]:
                load.wait()
            signal[tile] = v_inner[tile].astype(F32) * v_source[tile].astype(F32)
        for place, ref in enumerate((signal, v_taps)):
            parts = pack(lambda q: ref[tile, pl.ds(q, PER, stride=PHASES), :], e, lane_roll)
            for d in range(CTX):
                send[chunk, d, :, place * LANES : (place + 1) * LANES] = parts[d].astype(BF16)
        if chunk == 0:
            pl.semaphore_wait(barrier, CTX + 2)
        for k in far_first:
            a_copy(chunk, k).start()
        recv[chunk, me] = send[chunk, me]
        if chunk == 1:
            for load in loads[6:]:
                load.start()

    def b_copy(chunk, k):
        to = peer(k)
        return pltpu.make_async_remote_copy(
            src_ref=y_send.at[chunk, to],
            dst_ref=y_recv.at[chunk, me],
            send_sem=b_send.at[chunk],
            recv_sem=b_recv.at[chunk],
            device_id=(to, rank),
            device_id_type=MESH,
        )

    def convolve(chunk):
        all_of(recv, chunk, a_send, a_recv).wait_recv()
        if chunk == 0:
            for load in loads[6:12]:
                load.wait()
        arrived = recv[chunk].reshape(ROWS, 2 * LANES)
        arrived = jnp.concatenate([arrived, arrived], axis=0)
        starts = range(0, ROWS, BLOCK)
        staged = [
            (dot(v_row_f[start : start + BLOCK], arrived), dot(v_row_f[ROWS + start : ROWS + start + BLOCK], arrived))
            for start in starts
        ]
        spectra = []
        for start, (real, imag) in zip(starts, staged):
            cosine, sine = v_twid[0, start : start + BLOCK], v_twid[1, start : start + BLOCK]
            turned = []
            for place in (0, 1):
                re = real[:, place * LANES : (place + 1) * LANES]
                im = imag[:, place * LANES : (place + 1) * LANES]
                turned.append(jnp.concatenate([re * cosine - im * sine, re * sine + im * cosine], axis=1))
            spectra.append(dot3(jnp.concatenate(turned, axis=0), v_ph_f))
        backs = []
        for both in spectra:
            xr, xi = both[:BLOCK, :LANES], both[:BLOCK, LANES:]
            hr, hi = both[BLOCK:, :LANES], both[BLOCK:, LANES:]
            backs.append(dot3(jnp.concatenate([xr * hr - xi * hi, xr * hi + xi * hr], axis=1), v_ph_i))
        reals, imags = [], []
        for start, back in zip(starts, backs):
            re, im = back[:, :LANES], back[:, LANES:]
            cosine, sine = v_untwid[0, start : start + BLOCK], v_untwid[1, start : start + BLOCK]
            reals.append(jnp.concatenate(split(re * cosine - im * sine), axis=1))
            imags.append(jnp.concatenate(split(re * sine + im * cosine), axis=1))
        spectrum = jnp.concatenate(reals + imags, axis=0)
        spectrum = jnp.concatenate([spectrum, spectrum], axis=0)
        side_rows = SIDE * PER
        for pair in ((2, 1), (3, 0)):
            to_x = [lax.rem(x_me + dx, SIDE) for dx in pair]
            left = [v_row_i[pl.ds(pl.multiple_of(x * side_rows, side_rows), side_rows), :] for x in to_x]
            wide = dot(jnp.concatenate(left, axis=0), spectrum)
            y = (wide[:, :LANES] + wide[:, LANES:]).astype(BF16)
            for n, dx in enumerate(pair):
                block = y[n * side_rows : (n + 1) * side_rows].reshape(SIDE, PER, LANES)
                y_send[chunk, pl.ds(to_x[n] * SIDE, SIDE)] = block
                for dz in (2, 1, 3, 0):
                    if dx or dz:
                        b_copy(chunk, dx * SIDE + dz).start()
        y_recv[chunk, me] = y_send[chunk, me]

    def piece(ref, p):
        return ref.at[pl.ds(p * PIECE, PIECE)]

    def ring(chunk, name, p):
        frm, slot, column, device, index = {
            "up": (0, 1, 0, up, 0),
            "down": (0, 3, 0, down, 1),
            "far": ((1, 3)[p], 2, 0, (up, down)[p], 2),
            "cross": ((1, 3)[p], 2, 1, (up, down)[p], 3),
        }[name]
        return pltpu.make_async_remote_copy(
            src_ref=piece(gated.at[frm, column, chunk], p),
            dst_ref=piece(gated.at[slot, column, chunk], p),
            send_sem=c_send.at[index // 2],
            recv_sem=c_recv.at[chunk, index, p],
            device_id=(me, device),
            device_id_type=MESH,
        )

    def pair(chunk, slot, p, column=0):
        return pltpu.make_async_remote_copy(
            src_ref=piece(gated.at[slot, column, chunk], p),
            dst_ref=piece(gated.at[slot, 1 - column, chunk], p),
            send_sem=s_send.at[{0: 0, 1: 1, 3: 1, 2: 2}[slot]],
            recv_sem=s_recv.at[chunk, 0, slot] if slot in (0, 2) else s_recv.at[chunk, 1 + p, slot],
            device_id=(me, sibling),
            device_id_type=MESH,
        )

    def together(ref, send_sem, recv_sem):
        return pltpu.make_async_remote_copy(
            src_ref=ref,
            dst_ref=ref,
            send_sem=send_sem,
            recv_sem=recv_sem,
            device_id=(me, sibling),
            device_id_type=MESH,
        )

    first_core, second_core = core == 0, core == 1

    def prepare():
        for load in loads[12:14]:
            load.wait()
        for chunk in range(SUBS):
            tile, e = chunk // 2, chunk % 2
            lanes = slice(tile * LANES, (tile + 1) * LANES)
            gates[chunk] = halves(v_outer[:, lanes].astype(F32), e)
            skipped[chunk] = halves(v_skip[0:1, lanes] * signal[tile], e)

    def gate(chunk):
        all_of(y_recv, chunk, b_send, b_recv).wait_recv()
        parts = swap_groups([y_recv[chunk, d].astype(F32) for d in range(CTX)], lane_roll)
        for j in range(CTX):
            y_full[pl.ds(j, PER, stride=CTX), :] = parts[j]
        gated[0, 0, chunk] = (gates[chunk] * (y_full[...] + skipped[chunk])).astype(BF16)
        for p in (0, 1):
            ring(chunk, "up", p).start()
            ring(chunk, "down", 1 - p).start()
        for p in (0, 1):
            pair(chunk, 0, p).start()

    def near(chunk):
        for name, slot, p in (("up", 1, 0), ("down", 3, 1)):
            ring(chunk, name, p).wait_recv()
            pair(chunk, slot, p).start()

            @pl.when(second_core)
            def _(p=p):
                ring(chunk, "far", p).start()

        for name, slot, p in (("up", 1, 1), ("down", 3, 0)):
            ring(chunk, name, p).wait_recv()
            pair(chunk, slot, p).start()

    def cross(chunk):
        @pl.when(second_core)
        def _():
            for slot, p in ((1, 0), (3, 1)):
                pair(chunk, slot, p).wait_recv()
                ring(chunk, "cross", p).start()

    def far(chunk):
        @pl.when(second_core)
        def _():
            for column, name in enumerate(("far", "cross")):
                for p in (0, 1):
                    ring(chunk, name, p).wait_recv()
                    pair(chunk, 2, p, column).start()

    def arrived_pairs(chunk, slot):
        if slot == 0:
            together(gated.at[0, 1, chunk], s_send.at[0], s_recv.at[chunk, 0, 0]).wait_recv()
        elif slot == 2:

            @pl.when(first_core)
            def _():
                together(gated.at[2, :, chunk], s_send.at[0], s_recv.at[chunk, 0, 2]).wait_recv()

        else:
            ahead = 0 if slot == 1 else 1

            @pl.when(first_core)
            def _():
                pair(chunk, slot, ahead).wait_recv()

            pair(chunk, slot, 1 - ahead).wait_recv()

    def project(chunk, slot, first=False, last=False):
        arrived_pairs(chunk, slot)
        if chunk == 0 and slot == 0:
            loads[14].wait()
        y_from = lax.rem(y_me + SIDE - slot, SIDE)
        width = LANES // 2
        right = []
        for c in (core, 1 - core):
            start = pl.multiple_of((2 * y_from + c) * CH + chunk * width, width)
            right += [v_weight[pl.ds(start, width), :]] * 2
        left = jnp.concatenate([gated[slot, 0, chunk], gated[slot, 1, chunk]], axis=1)
        upper = lane_bit(left.shape, width)
        none = jnp.zeros_like(left)
        left = jnp.concatenate([jnp.where(upper, none, left), jnp.where(upper, left, none)], axis=0)
        term = dot(left, jnp.concatenate(right, axis=0))
        if not first:
            term = acc[...] + term
        if last:
            rows = term.astype(BF16).reshape(2, PER, PHASES // 2, FEATURES)
            for h in (0, 1):
                for r in range(PER):
                    start = r * PHASES + h * (PHASES // 2)
                    out[start : start + PHASES // 2] = rows[h, r]
        else:
            acc[...] = term

    prepare()
    for chunk in range(SUBS):
        convolve(chunk)
    for chunk in range(SUBS):
        gate(chunk)
    for chunk in range(SUBS):
        all_of(recv, chunk, a_send, a_recv).wait_send()
    near(0)
    for chunk in range(SUBS):
        all_of(y_recv, chunk, b_send, b_recv).wait_send()
    near(1)
    near(2)
    cross(0)
    project(0, 0, first=True)
    near(3)
    cross(1)
    project(1, 0)
    cross(2)
    far(0)
    project(2, 0)
    project(0, 1)
    project(0, 3)
    cross(3)
    far(1)
    project(3, 0)
    project(1, 1)
    project(1, 3)
    far(2)
    project(0, 2)
    project(2, 1)
    project(2, 3)
    far(3)
    project(1, 2)
    project(3, 1)
    project(3, 3)
    project(2, 2)
    project(3, 2, last=True)

    def sent(ref, send_sem):
        together(ref, send_sem, s_recv.at[0, 0, 0]).wait_send()

    sent(gated.at[0], c_send.at[0])
    sent(gated.at[0, 0], s_send.at[0])
    sent(gated.at[0], s_send.at[1])

    @pl.when(second_core)
    def _():
        sent(gated.at[0], c_send.at[1])
        sent(gated.at[0], s_send.at[2])


def on_device(inner_gate, outer_gate, source_values, filter_taps, skip_gain, output_weight):
    constants = [jnp.asarray(table) for table in tables()]
    operands = (inner_gate, outer_gate, source_values, filter_taps, skip_gain.reshape(1, CH), output_weight, *constants)
    vmem = pltpu.VMEM
    dma = pltpu.SemaphoreType.DMA
    return pl.pallas_call(
        kernel,
        out_shape=jax.ShapeDtypeStruct((TOK, FEATURES), BF16),
        in_specs=[pl.BlockSpec(memory_space=pltpu.HBM)] * len(operands),
        out_specs=pl.BlockSpec(memory_space=pltpu.VMEM),
        scratch_shapes=[
            vmem((TILES, TOK, LANES), BF16),
            vmem((TOK, CH), BF16),
            vmem((TILES, TOK, LANES), BF16),
            vmem((TILES, TOK, LANES), F32),
            vmem((1, CH), F32),
            vmem((output_weight.shape[0], FEATURES), BF16),
            *[vmem(table.shape, table.dtype) for table in constants],
            vmem((TILES, TOK, LANES), F32),
            vmem((SUBS, CTX, PER, 2 * LANES), BF16),
            vmem((SUBS, CTX, PER, 2 * LANES), BF16),
            vmem((SUBS, CTX, PER, LANES), BF16),
            vmem((SUBS, CTX, PER, LANES), BF16),
            vmem((HALF, LANES), F32),
            vmem((SUBS, HALF, LANES), F32),
            vmem((SUBS, HALF, LANES), F32),
            vmem((SIDE, 2, SUBS, HALF, LANES), BF16),
            vmem((TOK, FEATURES), F32),
            dma((15,)),
            dma((SUBS,)),
            dma((SUBS,)),
            dma((SUBS,)),
            dma((SUBS,)),
            dma((2,)),
            dma((SUBS, 4, 2)),
            dma((3,)),
            dma((SUBS, 3, SIDE)),
        ],
        compiler_params=pltpu.CompilerParams(
            collective_id=0, has_side_effects=True, vmem_limit_bytes=48 * 1024 * 1024
        ),
        cost_estimate=pl.CostEstimate(flops=3 * 10**9, bytes_accessed=8 * 10**6, transcendentals=0),
        name="hyena",
    )(*[pltpu.with_memory_space_constraint(operand, pltpu.HBM) for operand in operands])


def solution(mesh):
    in_specs = (P("ctx", "ch"), P("ctx", "ch"), P("ctx", "ch"), P("ctx", "ch"), P("ch"), P())
    out_specs = P("ctx", "ch")
    return jax.shard_map(
        on_device, mesh=mesh, in_specs=in_specs, out_specs=out_specs, check_vma=False
    )
```

```python
import functools

import jax
import jax.numpy as jnp
import ml_dtypes
import numpy as np
from jax import lax
from jax.experimental import pallas as pl
from jax.experimental.pallas import tpu as pltpu
from jax.sharding import PartitionSpec as P

MESH = pl.DeviceIdType.MESH
F32 = jnp.float32
BF16 = jnp.bfloat16

CTX = 16
SIDE = 4
TOK = 512
CH = 256
LANES = 128
TILES = 2
SUBS = 4
GROUP = 4
PHASES = 32
PER = TOK // PHASES
ROWS = CTX * PER
LENGTH = ROWS * PHASES
FEATURES = 256
HALF = TOK // 2
PIECE = HALF // 2
BLOCK = 128


def split_table(table, axis):
    high = table.astype(np.float32).astype(ml_dtypes.bfloat16)
    low = (table - high.astype(np.float64)).astype(np.float32).astype(ml_dtypes.bfloat16)
    if axis == 1:
        return np.concatenate([high, low], axis=1)
    return np.concatenate([high, high, low], axis=0)


def tables():
    k_row = np.arange(ROWS) + 0.25
    rows = np.arange(ROWS)
    turn = 2.0 * np.pi * np.outer(k_row, rows) / ROWS
    row_forward = np.concatenate([np.cos(turn), -np.sin(turn)], axis=0)
    row_inverse = np.concatenate([np.cos(turn.T), -np.sin(turn.T)], axis=1)
    phase = np.repeat(np.arange(PHASES), GROUP)
    twist = 2.0 * np.pi * np.outer(k_row, phase) / LENGTH
    twiddle = np.stack([np.cos(twist), -np.sin(twist)]).astype(np.float32)
    untwiddle = (np.stack([np.cos(twist), np.sin(twist)]) / LENGTH).astype(np.float32)
    angle = 2.0 * np.pi * np.outer(np.arange(PHASES), np.arange(PHASES)) / PHASES
    cosine = np.kron(np.cos(angle), np.eye(GROUP))
    sine = np.kron(np.sin(angle), np.eye(GROUP))
    phase_forward = np.block([[cosine, -sine], [sine, cosine]])
    phase_inverse = np.block([[cosine, sine], [-sine, cosine]])
    return (
        split_table(row_forward, 1),
        split_table(row_inverse, 1),
        twiddle,
        untwiddle,
        split_table(phase_forward, 0),
        split_table(phase_inverse, 0),
    )


def lane_bit(shape, width):
    return (lax.broadcasted_iota(jnp.int32, shape, 1) & width) != 0


def swap_groups(parts, roll):
    parts = list(parts)
    bit = CTX // 2
    while bit:
        shift = bit * GROUP
        upper = lane_bit(parts[0].shape, shift)
        for j in range(CTX):
            if j & bit:
                continue
            first, second = parts[j], parts[j | bit]
            parts[j] = jnp.where(upper, roll(second, shift), first)
            parts[j | bit] = jnp.where(upper, second, roll(first, LANES - shift))
        bit //= 2
    return parts


def pack(rows_of, e, roll):
    parts = []
    for j in range(CTX):
        first, second = rows_of(j), rows_of(j + CTX)
        upper = lane_bit(first.shape, LANES // 2)
        if e == 0:
            parts.append(jnp.where(upper, roll(second, LANES // 2), first))
        else:
            parts.append(jnp.where(upper, second, roll(first, LANES // 2)))
    return swap_groups(parts, roll)


def halves(rows, e):
    blocks = rows.reshape(PER, 2, PHASES // 2, LANES)
    first, second = blocks[:, 0].reshape(HALF, LANES), blocks[:, 1].reshape(HALF, LANES)
    upper = lane_bit(first.shape, LANES // 2)
    if e == 0:
        return jnp.where(upper, pltpu.roll(second, LANES // 2, 1), first)
    return jnp.where(upper, second, pltpu.roll(first, LANES // 2, 1))


def lane_roll(value, shift):
    return pltpu.roll(value, shift, 1)


def split(value):
    high = value.astype(BF16)
    return high, (value - high.astype(F32)).astype(BF16)


def dot(a, b):
    return jnp.dot(a, b, preferred_element_type=F32)


def dot3(value, table):
    high, low = split(value)
    return dot(jnp.concatenate([high, low, high], axis=1), table[...])


def kernel(
    inner, outer, source, taps, skip, weight, row_f, row_i, twid, untwid, ph_f, ph_i,
    out,
    v_inner, v_outer, v_source, v_taps, v_skip, v_weight, v_row_f, v_row_i, v_twid, v_untwid, v_ph_f, v_ph_i,
    signal, send, recv, y_send, y_recv, y_full, gates, skipped, gated, acc,
    load_sem, a_send, a_recv, b_send, b_recv, c_send, c_recv, s_send, s_recv,
):
    me = lax.axis_index("ctx")
    rank = lax.axis_index("ch")
    x_me, z_me = me // SIDE, me % SIDE
    y_me, core = rank // 2, rank % 2
    up = lax.rem(y_me + 1, SIDE) * 2 + core
    down = lax.rem(y_me + SIDE - 1, SIDE) * 2 + core
    sibling = y_me * 2 + (1 - core)

    def peer(k):
        return lax.rem(x_me + k // SIDE, SIDE) * SIDE + lax.rem(z_me + k % SIDE, SIDE)

    feature0 = pl.multiple_of(rank * FEATURES, FEATURES)
    pairs = []
    for tile in range(TILES):
        lanes = pl.ds(tile * LANES, LANES)
        pairs += [(src.at[:, lanes], dst.at[tile]) for src, dst in ((taps, v_taps), (inner, v_inner), (source, v_source))]
    pairs += [(row_f, v_row_f), (twid, v_twid), (ph_f, v_ph_f), (ph_i, v_ph_i), (untwid, v_untwid), (row_i, v_row_i)]
    pairs += [(outer, v_outer), (skip, v_skip), (weight.at[:, pl.ds(feature0, FEATURES)], v_weight)]
    loads = [pltpu.make_async_copy(src, dst, load_sem.at[n]) for n, (src, dst) in enumerate(pairs)]
    for load in loads[:6]:
        load.start()

    barrier = pltpu.get_barrier_semaphore()
    for k in range(1, CTX):
        pl.semaphore_signal(barrier, inc=1, device_id=(peer(k), rank), device_id_type=MESH)
    for other in (up, down, sibling):
        pl.semaphore_signal(barrier, inc=1, device_id=(me, other), device_id_type=MESH)

    far_first = sorted(range(1, CTX), key=lambda k: -(2 - abs(2 - k // SIDE)) - (2 - abs(2 - k % SIDE)))

    def all_of(ref, chunk, send_sem, recv_sem):
        ref = ref.at[chunk, pl.ds(0, CTX - 1)]
        return pltpu.make_async_remote_copy(
            src_ref=ref,
            dst_ref=ref,
            send_sem=send_sem.at[0],
            recv_sem=recv_sem.at[chunk],
            device_id=(me, sibling),
            device_id_type=MESH,
        )

    def a_copy(chunk, k):
        to = peer(k)
        return pltpu.make_async_remote_copy(
            src_ref=send.at[chunk, to],
            dst_ref=recv.at[chunk, me],
            send_sem=a_send.at[0],
            recv_sem=a_recv.at[chunk],
            device_id=(to, rank),
            device_id_type=MESH,
        )

    for chunk in range(SUBS):
        tile, e = chunk // 2, chunk % 2
        if e == 0:
            for load in loads[3 * tile : 3 * tile + 3]:
                load.wait()
            signal[tile] = v_inner[tile].astype(F32) * v_source[tile].astype(F32)
        for place, ref in enumerate((signal, v_taps)):
            parts = pack(lambda q: ref[tile, pl.ds(q, PER, stride=PHASES), :], e, lane_roll)
            for d in range(CTX):
                send[chunk, d, :, place * LANES : (place + 1) * LANES] = parts[d].astype(BF16)
        if chunk == 0:
            pl.semaphore_wait(barrier, CTX + 2)
        for k in far_first:
            a_copy(chunk, k).start()
        recv[chunk, me] = send[chunk, me]
        if chunk == 1:
            for load in loads[6:]:
                load.start()

    def b_copy(chunk, k):
        to = peer(k)
        return pltpu.make_async_remote_copy(
            src_ref=y_send.at[chunk, to],
            dst_ref=y_recv.at[chunk, me],
            send_sem=b_send.at[0],
            recv_sem=b_recv.at[chunk],
            device_id=(to, rank),
            device_id_type=MESH,
        )

    def convolve(chunk):
        all_of(recv, chunk, a_send, a_recv).wait_recv()
        if chunk == 0:
            for load in loads[6:12]:
                load.wait()
        arrived = recv[chunk].reshape(ROWS, 2 * LANES)
        arrived = jnp.concatenate([arrived, arrived], axis=0)
        starts = range(0, ROWS, BLOCK)
        staged = [
            (dot(v_row_f[start : start + BLOCK], arrived), dot(v_row_f[ROWS + start : ROWS + start + BLOCK], arrived))
            for start in starts
        ]
        spectra = []
        for start, (real, imag) in zip(starts, staged):
            cosine, sine = v_twid[0, start : start + BLOCK], v_twid[1, start : start + BLOCK]
            turned = []
            for place in (0, 1):
                re = real[:, place * LANES : (place + 1) * LANES]
                im = imag[:, place * LANES : (place + 1) * LANES]
                turned.append(jnp.concatenate([re * cosine - im * sine, re * sine + im * cosine], axis=1))
            spectra.append(dot3(jnp.concatenate(turned, axis=0), v_ph_f))
        backs = []
        for both in spectra:
            xr, xi = both[:BLOCK, :LANES], both[:BLOCK, LANES:]
            hr, hi = both[BLOCK:, :LANES], both[BLOCK:, LANES:]
            backs.append(dot3(jnp.concatenate([xr * hr - xi * hi, xr * hi + xi * hr], axis=1), v_ph_i))
        reals, imags = [], []
        for start, back in zip(starts, backs):
            re, im = back[:, :LANES], back[:, LANES:]
            cosine, sine = v_untwid[0, start : start + BLOCK], v_untwid[1, start : start + BLOCK]
            reals.append(jnp.concatenate(split(re * cosine - im * sine), axis=1))
            imags.append(jnp.concatenate(split(re * sine + im * cosine), axis=1))
        spectrum = jnp.concatenate(reals + imags, axis=0)
        spectrum = jnp.concatenate([spectrum, spectrum], axis=0)
        side_rows = SIDE * PER
        for pair in ((2, 1), (3, 0)):
            to_x = [lax.rem(x_me + dx, SIDE) for dx in pair]
            left = [v_row_i[pl.ds(pl.multiple_of(x * side_rows, side_rows), side_rows), :] for x in to_x]
            wide = dot(jnp.concatenate(left, axis=0), spectrum)
            y = (wide[:, :LANES] + wide[:, LANES:]).astype(BF16)
            for n, dx in enumerate(pair):
                block = y[n * side_rows : (n + 1) * side_rows].reshape(SIDE, PER, LANES)
                y_send[chunk, pl.ds(to_x[n] * SIDE, SIDE)] = block
                for dz in (2, 1, 3, 0):
                    if dx or dz:
                        b_copy(chunk, dx * SIDE + dz).start()
        y_recv[chunk, me] = y_send[chunk, me]

    def piece(ref, p):
        return ref.at[pl.ds(p * PIECE, PIECE)]

    def ring(chunk, name, p):
        frm, slot, column, device, index = {
            "up": (0, 1, 0, up, 0),
            "down": (0, 3, 0, down, 1),
            "far": ((1, 3)[p], 2, 0, (up, down)[p], 2),
            "cross": ((1, 3)[p], 2, 1, (up, down)[p], 3),
        }[name]
        return pltpu.make_async_remote_copy(
            src_ref=piece(gated.at[frm, column, chunk], p),
            dst_ref=piece(gated.at[slot, column, chunk], p),
            send_sem=c_send.at[index // 2],
            recv_sem=c_recv.at[chunk, 4 if index >= 2 else 2 * index + p],
            device_id=(me, device),
            device_id_type=MESH,
        )

    def pair(chunk, slot, p, column=0):
        return pltpu.make_async_remote_copy(
            src_ref=piece(gated.at[slot, column, chunk], p),
            dst_ref=piece(gated.at[slot, 1 - column, chunk], p),
            send_sem=s_send.at[{0: 0, 1: 1, 3: 1, 2: 2}[slot]],
            recv_sem=s_recv.at[chunk, slot // 2 if slot in (0, 2) else slot + 1 + p],
            device_id=(me, sibling),
            device_id_type=MESH,
        )

    def together(ref, send_sem, recv_sem):
        return pltpu.make_async_remote_copy(
            src_ref=ref,
            dst_ref=ref,
            send_sem=send_sem,
            recv_sem=recv_sem,
            device_id=(me, sibling),
            device_id_type=MESH,
        )

    first_core, second_core = core == 0, core == 1

    def prepare():
        for load in loads[12:14]:
            load.wait()
        for chunk in range(SUBS):
            tile, e = chunk // 2, chunk % 2
            lanes = slice(tile * LANES, (tile + 1) * LANES)
            gates[chunk] = halves(v_outer[:, lanes].astype(F32), e)
            skipped[chunk] = halves(v_skip[0:1, lanes] * signal[tile], e)

    def gate(chunk):
        all_of(y_recv, chunk, b_send, b_recv).wait_recv()
        parts = swap_groups([y_recv[chunk, d].astype(F32) for d in range(CTX)], lane_roll)
        for j in range(CTX):
            y_full[pl.ds(j, PER, stride=CTX), :] = parts[j]
        gated[0, 0, chunk] = (gates[chunk] * (y_full[...] + skipped[chunk])).astype(BF16)
        for p in (0, 1):
            ring(chunk, "up", p).start()
            ring(chunk, "down", 1 - p).start()
        for p in (0, 1):
            pair(chunk, 0, p).start()

    def near(chunk):
        for name, slot, p in (("up", 1, 0), ("down", 3, 1)):
            ring(chunk, name, p).wait_recv()
            pair(chunk, slot, p).start()

            @pl.when(second_core)
            def _(p=p):
                ring(chunk, "far", p).start()

        for name, slot, p in (("up", 1, 1), ("down", 3, 0)):
            ring(chunk, name, p).wait_recv()
            pair(chunk, slot, p).start()

    def cross(chunk):
        @pl.when(second_core)
        def _():
            for slot, p in ((1, 0), (3, 1)):
                pair(chunk, slot, p).wait_recv()
                ring(chunk, "cross", p).start()

    def far(chunk):
        @pl.when(second_core)
        def _():
            together(gated.at[2, :, chunk], c_send.at[0], c_recv.at[chunk, 4]).wait_recv()
            for column in (0, 1):
                for p in (0, 1):
                    pair(chunk, 2, p, column).start()

    def arrived_pairs(chunk, slot):
        if slot == 0:
            together(gated.at[0, 1, chunk], s_send.at[0], s_recv.at[chunk, 0]).wait_recv()
        elif slot == 2:

            @pl.when(first_core)
            def _():
                together(gated.at[2, :, chunk], s_send.at[0], s_recv.at[chunk, 1]).wait_recv()

        else:
            ahead = 0 if slot == 1 else 1

            @pl.when(first_core)
            def _():
                pair(chunk, slot, ahead).wait_recv()

            pair(chunk, slot, 1 - ahead).wait_recv()

    def project(items, first=False, last=False):
        lefts, rights = [], []
        for chunk, slot in items:
            arrived_pairs(chunk, slot)
            if chunk == 0 and slot == 0:
                loads[14].wait()
            y_from = lax.rem(y_me + SIDE - slot, SIDE)
            width = LANES // 2
            for c in (core, 1 - core):
                start = pl.multiple_of((2 * y_from + c) * CH + chunk * width, width)
                rights += [v_weight[pl.ds(start, width), :]] * 2
            lefts += [gated[slot, 0, chunk], gated[slot, 1, chunk]]
        left = jnp.concatenate(lefts, axis=1)
        upper = lane_bit(left.shape, LANES // 2)
        none = jnp.zeros_like(left)
        left = jnp.concatenate([jnp.where(upper, none, left), jnp.where(upper, left, none)], axis=0)
        term = dot(left, jnp.concatenate(rights, axis=0))
        if not first:
            term = acc[...] + term
        if last:
            rows = term.astype(BF16).reshape(2, PER, PHASES // 2, FEATURES)
            for h in (0, 1):
                for r in range(PER):
                    start = r * PHASES + h * (PHASES // 2)
                    out[start : start + PHASES // 2] = rows[h, r]
        else:
            acc[...] = term

    prepare()
    for chunk in range(SUBS):
        convolve(chunk)
    for chunk in range(SUBS):
        gate(chunk)
    together(recv.at[:, pl.ds(0, CTX - 1)], a_send.at[0], s_recv.at[0, 0]).wait_send()
    near(0)
    together(y_recv.at[:, pl.ds(0, CTX - 1)], b_send.at[0], s_recv.at[0, 0]).wait_send()
    near(1)
    near(2)
    cross(0)
    project([(0, 0)], first=True)
    near(3)
    cross(1)
    project([(1, 0)])
    cross(2)
    far(0)
    project([(2, 0), (0, 1), (0, 3)])
    cross(3)
    far(1)
    project([(3, 0), (1, 1), (1, 3)])
    far(2)
    project([(0, 2), (2, 1), (2, 3)])
    far(3)
    project([(1, 2), (3, 1), (3, 3)])
    project([(2, 2), (3, 2)], last=True)

    def sent(ref, send_sem):
        together(ref, send_sem, s_recv.at[0, 0]).wait_send()

    sent(gated.at[0], c_send.at[0])
    sent(gated.at[0, 0], s_send.at[0])
    sent(gated.at[0], s_send.at[1])

    @pl.when(second_core)
    def _():
        sent(gated.at[0], c_send.at[1])
        sent(gated.at[0], s_send.at[2])


def on_device(inner_gate, outer_gate, source_values, filter_taps, skip_gain, output_weight):
    constants = [jnp.asarray(table) for table in tables()]
    operands = (inner_gate, outer_gate, source_values, filter_taps, skip_gain.reshape(1, CH), output_weight, *constants)
    vmem = pltpu.VMEM
    dma = pltpu.SemaphoreType.DMA
    return pl.pallas_call(
        kernel,
        out_shape=jax.ShapeDtypeStruct((TOK, FEATURES), BF16),
        in_specs=[pl.BlockSpec(memory_space=pltpu.HBM)] * len(operands),
        out_specs=pl.BlockSpec(memory_space=pltpu.VMEM),
        scratch_shapes=[
            vmem((TILES, TOK, LANES), BF16),
            vmem((TOK, CH), BF16),
            vmem((TILES, TOK, LANES), BF16),
            vmem((TILES, TOK, LANES), F32),
            vmem((1, CH), F32),
            vmem((output_weight.shape[0], FEATURES), BF16),
            *[vmem(table.shape, table.dtype) for table in constants],
            vmem((TILES, TOK, LANES), F32),
            vmem((SUBS, CTX, PER, 2 * LANES), BF16),
            vmem((SUBS, CTX, PER, 2 * LANES), BF16),
            vmem((SUBS, CTX, PER, LANES), BF16),
            vmem((SUBS, CTX, PER, LANES), BF16),
            vmem((HALF, LANES), F32),
            vmem((SUBS, HALF, LANES), F32),
            vmem((SUBS, HALF, LANES), F32),
            vmem((SIDE, 2, SUBS, HALF, LANES), BF16),
            vmem((TOK, FEATURES), F32),
            dma((15,)),
            dma((1,)),
            dma((SUBS,)),
            dma((1,)),
            dma((SUBS,)),
            dma((2,)),
            dma((SUBS, 5)),
            dma((3,)),
            dma((SUBS, 6)),
        ],
        compiler_params=pltpu.CompilerParams(
            collective_id=0, has_side_effects=True, vmem_limit_bytes=48 * 1024 * 1024
        ),
        cost_estimate=pl.CostEstimate(flops=3 * 10**9, bytes_accessed=8 * 10**6, transcendentals=0),
        name="hyena",
    )(*[pltpu.with_memory_space_constraint(operand, pltpu.HBM) for operand in operands])


def solution(mesh):
    in_specs = (P("ctx", "ch"), P("ctx", "ch"), P("ctx", "ch"), P("ctx", "ch"), P("ch"), P())
    out_specs = P("ctx", "ch")
    return jax.shard_map(
        on_device, mesh=mesh, in_specs=in_specs, out_specs=out_specs, check_vma=False
    )
```

```python
import functools

import jax
import jax.numpy as jnp
import ml_dtypes
import numpy as np
from jax import lax
from jax.experimental import pallas as pl
from jax.experimental.pallas import tpu as pltpu
from jax.sharding import PartitionSpec as P

MESH = pl.DeviceIdType.MESH
F32 = jnp.float32
BF16 = jnp.bfloat16

CTX = 16
SIDE = 4
TOK = 512
CH = 256
LANES = 128
TILES = 2
SUBS = 4
GROUP = 4
PHASES = 32
PER = TOK // PHASES
ROWS = CTX * PER
LENGTH = ROWS * PHASES
FEATURES = 256
HALF = TOK // 2
PIECE = HALF // 2
BLOCK = 128


def split_table(table, axis):
    high = table.astype(np.float32).astype(ml_dtypes.bfloat16)
    low = (table - high.astype(np.float64)).astype(np.float32).astype(ml_dtypes.bfloat16)
    if axis == 1:
        return np.concatenate([high, low], axis=1)
    return np.concatenate([high, high, low], axis=0)


def tables():
    k_row = np.arange(ROWS) + 0.25
    rows = np.arange(ROWS)
    turn = 2.0 * np.pi * np.outer(k_row, rows) / ROWS
    row_forward = np.concatenate([np.cos(turn), -np.sin(turn)], axis=0)
    row_inverse = np.concatenate([np.cos(turn.T), -np.sin(turn.T)], axis=1)
    phase = np.repeat(np.arange(PHASES), GROUP)
    twist = 2.0 * np.pi * np.outer(k_row, phase) / LENGTH
    twiddle = np.stack([np.cos(twist), -np.sin(twist)]).astype(np.float32)
    untwiddle = (np.stack([np.cos(twist), np.sin(twist)]) / LENGTH).astype(np.float32)
    angle = 2.0 * np.pi * np.outer(np.arange(PHASES), np.arange(PHASES)) / PHASES
    cosine = np.kron(np.cos(angle), np.eye(GROUP))
    sine = np.kron(np.sin(angle), np.eye(GROUP))
    phase_forward = np.block([[cosine, -sine], [sine, cosine]])
    phase_inverse = np.block([[cosine, sine], [-sine, cosine]])
    return (
        split_table(row_forward, 1),
        split_table(row_inverse, 1),
        twiddle,
        untwiddle,
        split_table(phase_forward, 0),
        split_table(phase_inverse, 0),
    )


def lane_bit(shape, width):
    return (lax.broadcasted_iota(jnp.int32, shape, 1) & width) != 0


def swap_groups(parts, roll):
    parts = list(parts)
    bit = CTX // 2
    while bit:
        shift = bit * GROUP
        upper = lane_bit(parts[0].shape, shift)
        for j in range(CTX):
            if j & bit:
                continue
            first, second = parts[j], parts[j | bit]
            parts[j] = jnp.where(upper, roll(second, shift), first)
            parts[j | bit] = jnp.where(upper, second, roll(first, LANES - shift))
        bit //= 2
    return parts


def pack(rows_of, e, roll):
    parts = []
    for j in range(CTX):
        first, second = rows_of(j), rows_of(j + CTX)
        upper = lane_bit(first.shape, LANES // 2)
        if e == 0:
            parts.append(jnp.where(upper, roll(second, LANES // 2), first))
        else:
            parts.append(jnp.where(upper, second, roll(first, LANES // 2)))
    return swap_groups(parts, roll)


def halves(rows, e):
    blocks = rows.reshape(PER, 2, PHASES // 2, LANES)
    first, second = blocks[:, 0].reshape(HALF, LANES), blocks[:, 1].reshape(HALF, LANES)
    upper = lane_bit(first.shape, LANES // 2)
    if e == 0:
        return jnp.where(upper, pltpu.roll(second, LANES // 2, 1), first)
    return jnp.where(upper, second, pltpu.roll(first, LANES // 2, 1))


def lane_roll(value, shift):
    return pltpu.roll(value, shift, 1)


def split(value):
    high = value.astype(BF16)
    return high, (value - high.astype(F32)).astype(BF16)


def dot(a, b):
    return jnp.dot(a, b, preferred_element_type=F32)


def dot3(value, table):
    high, low = split(value)
    return dot(jnp.concatenate([high, low, high], axis=1), table[...])


def kernel(
    inner, outer, source, taps, skip, weight, row_f, row_i, twid, untwid, ph_f, ph_i,
    out,
    v_inner, v_outer, v_source, v_taps, v_skip, v_weight, v_row_f, v_row_i, v_twid, v_untwid, v_ph_f, v_ph_i,
    signal, send, recv, y_send, y_recv, y_full, gates, skipped, gated, acc,
    load_sem, a_send, a_recv, b_send, b_recv, c_send, c_recv, s_send, s_recv,
):
    me = lax.axis_index("ctx")
    rank = lax.axis_index("ch")
    x_me, z_me = me // SIDE, me % SIDE
    y_me, core = rank // 2, rank % 2
    up = lax.rem(y_me + 1, SIDE) * 2 + core
    down = lax.rem(y_me + SIDE - 1, SIDE) * 2 + core
    sibling = y_me * 2 + (1 - core)

    def peer(k):
        return lax.rem(x_me + k // SIDE, SIDE) * SIDE + lax.rem(z_me + k % SIDE, SIDE)

    feature0 = pl.multiple_of(rank * FEATURES, FEATURES)
    pairs = []
    for tile in range(TILES):
        lanes = pl.ds(tile * LANES, LANES)
        pairs += [(src.at[:, lanes], dst.at[tile]) for src, dst in ((taps, v_taps), (inner, v_inner), (source, v_source))]
    pairs += [(row_f, v_row_f), (twid, v_twid), (ph_f, v_ph_f), (ph_i, v_ph_i), (untwid, v_untwid), (row_i, v_row_i)]
    pairs += [(outer, v_outer), (skip, v_skip), (weight.at[:, pl.ds(feature0, FEATURES)], v_weight)]
    loads = [pltpu.make_async_copy(src, dst, load_sem.at[n]) for n, (src, dst) in enumerate(pairs)]
    for load in loads[:6]:
        load.start()

    barrier = pltpu.get_barrier_semaphore()
    for k in range(1, CTX):
        pl.semaphore_signal(barrier, inc=1, device_id=(peer(k), rank), device_id_type=MESH)
    for other in (up, down, sibling):
        pl.semaphore_signal(barrier, inc=1, device_id=(me, other), device_id_type=MESH)

    far_first = sorted(range(1, CTX), key=lambda k: -(2 - abs(2 - k // SIDE)) - (2 - abs(2 - k % SIDE)))

    def all_of(ref, chunk, send_sem, recv_sem):
        ref = ref.at[chunk, pl.ds(0, CTX - 1)]
        return pltpu.make_async_remote_copy(
            src_ref=ref,
            dst_ref=ref,
            send_sem=send_sem.at[0],
            recv_sem=recv_sem.at[chunk],
            device_id=(me, sibling),
            device_id_type=MESH,
        )

    def a_copy(chunk, k):
        to = peer(k)
        return pltpu.make_async_remote_copy(
            src_ref=send.at[chunk, to],
            dst_ref=recv.at[chunk, me],
            send_sem=a_send.at[0],
            recv_sem=a_recv.at[chunk],
            device_id=(to, rank),
            device_id_type=MESH,
        )

    for chunk in range(SUBS):
        tile, e = chunk // 2, chunk % 2
        if e == 0:
            for load in loads[3 * tile : 3 * tile + 3]:
                load.wait()
            signal[tile] = v_inner[tile].astype(F32) * v_source[tile].astype(F32)
        for place, ref in enumerate((signal, v_taps)):
            parts = pack(lambda q: ref[tile, pl.ds(q, PER, stride=PHASES), :], e, lane_roll)
            for d in range(CTX):
                send[chunk, d, :, place * LANES : (place + 1) * LANES] = parts[d].astype(BF16)
        if chunk == 0:
            pl.semaphore_wait(barrier, CTX + 2)
        for k in far_first:
            a_copy(chunk, k).start()
        recv[chunk, me] = send[chunk, me]
        if chunk == 1:
            for load in loads[6:]:
                load.start()

    def b_copy(chunk, k):
        to = peer(k)
        return pltpu.make_async_remote_copy(
            src_ref=y_send.at[chunk, to],
            dst_ref=y_recv.at[chunk, me],
            send_sem=b_send.at[0],
            recv_sem=b_recv.at[chunk],
            device_id=(to, rank),
            device_id_type=MESH,
        )

    def convolve(chunk):
        all_of(recv, chunk, a_send, a_recv).wait_recv()
        if chunk == 0:
            for load in loads[6:12]:
                load.wait()
        arrived = recv[chunk].reshape(ROWS, 2 * LANES)
        arrived = jnp.concatenate([arrived, arrived], axis=0)
        starts = range(0, ROWS, BLOCK)
        staged = [
            (dot(v_row_f[start : start + BLOCK], arrived), dot(v_row_f[ROWS + start : ROWS + start + BLOCK], arrived))
            for start in starts
        ]
        spectra = []
        for start, (real, imag) in zip(starts, staged):
            cosine, sine = v_twid[0, start : start + BLOCK], v_twid[1, start : start + BLOCK]
            turned = []
            for place in (0, 1):
                re = real[:, place * LANES : (place + 1) * LANES]
                im = imag[:, place * LANES : (place + 1) * LANES]
                turned.append(jnp.concatenate([re * cosine - im * sine, re * sine + im * cosine], axis=1))
            spectra.append(dot3(jnp.concatenate(turned, axis=0), v_ph_f))
        backs = []
        for both in spectra:
            xr, xi = both[:BLOCK, :LANES], both[:BLOCK, LANES:]
            hr, hi = both[BLOCK:, :LANES], both[BLOCK:, LANES:]
            backs.append(dot3(jnp.concatenate([xr * hr - xi * hi, xr * hi + xi * hr], axis=1), v_ph_i))
        reals, imags = [], []
        for start, back in zip(starts, backs):
            re, im = back[:, :LANES], back[:, LANES:]
            cosine, sine = v_untwid[0, start : start + BLOCK], v_untwid[1, start : start + BLOCK]
            reals.append(jnp.concatenate(split(re * cosine - im * sine), axis=1))
            imags.append(jnp.concatenate(split(re * sine + im * cosine), axis=1))
        spectrum = jnp.concatenate(reals + imags, axis=0)
        spectrum = jnp.concatenate([spectrum, spectrum], axis=0)
        side_rows = SIDE * PER
        for pair in ((2, 1), (3, 0)):
            to_x = [lax.rem(x_me + dx, SIDE) for dx in pair]
            left = [v_row_i[pl.ds(pl.multiple_of(x * side_rows, side_rows), side_rows), :] for x in to_x]
            wide = dot(jnp.concatenate(left, axis=0), spectrum)
            y = (wide[:, :LANES] + wide[:, LANES:]).astype(BF16)
            for n, dx in enumerate(pair):
                block = y[n * side_rows : (n + 1) * side_rows].reshape(SIDE, PER, LANES)
                y_send[chunk, pl.ds(to_x[n] * SIDE, SIDE)] = block
                for dz in (2, 1, 3, 0):
                    if dx or dz:
                        b_copy(chunk, dx * SIDE + dz).start()
        y_recv[chunk, me] = y_send[chunk, me]

    def piece(ref, p):
        return ref.at[pl.ds(p * PIECE, PIECE)]

    def ring(chunk, name, p):
        frm, slot, column, device, index = {
            "up": (0, 1, 0, up, 0),
            "down": (0, 3, 0, down, 1),
            "far": ((1, 3)[p], 2, 0, (up, down)[p], 2),
            "cross": ((1, 3)[p], 2, 1, (up, down)[p], 3),
        }[name]
        return pltpu.make_async_remote_copy(
            src_ref=piece(gated.at[frm, column, chunk], p),
            dst_ref=piece(gated.at[slot, column, chunk], p),
            send_sem=c_send.at[index // 2],
            recv_sem=c_recv.at[chunk, 3 if index >= 2 else 2 * index if p == index else 1],
            device_id=(me, device),
            device_id_type=MESH,
        )

    def pair(chunk, slot, p, column=0):
        return pltpu.make_async_remote_copy(
            src_ref=piece(gated.at[slot, column, chunk], p),
            dst_ref=piece(gated.at[slot, 1 - column, chunk], p),
            send_sem=s_send.at[{0: 0, 1: 1, 3: 1, 2: 2}[slot]],
            recv_sem=s_recv.at[chunk, slot // 2 if slot in (0, 2) else slot + 1 + p],
            device_id=(me, sibling),
            device_id_type=MESH,
        )

    def together(ref, send_sem, recv_sem):
        return pltpu.make_async_remote_copy(
            src_ref=ref,
            dst_ref=ref,
            send_sem=send_sem,
            recv_sem=recv_sem,
            device_id=(me, sibling),
            device_id_type=MESH,
        )

    first_core, second_core = core == 0, core == 1

    def prepare():
        for load in loads[12:14]:
            load.wait()
        for chunk in range(SUBS):
            tile, e = chunk // 2, chunk % 2
            lanes = slice(tile * LANES, (tile + 1) * LANES)
            gates[chunk] = halves(v_outer[:, lanes].astype(F32), e)
            skipped[chunk] = halves(v_skip[0:1, lanes] * signal[tile], e)

    def gate(chunk):
        all_of(y_recv, chunk, b_send, b_recv).wait_recv()
        parts = swap_groups([y_recv[chunk, d].astype(F32) for d in range(CTX)], lane_roll)
        for j in range(CTX):
            y_full[pl.ds(j, PER, stride=CTX), :] = parts[j]
        gated[0, 0, chunk] = (gates[chunk] * (y_full[...] + skipped[chunk])).astype(BF16)
        for p in (0, 1):
            ring(chunk, "up", p).start()
            ring(chunk, "down", 1 - p).start()
        for p in (0, 1):
            pair(chunk, 0, p).start()

    def near(chunk):
        for name, slot, p in (("up", 1, 0), ("down", 3, 1)):
            ring(chunk, name, p).wait_recv()
            pair(chunk, slot, p).start()

            @pl.when(second_core)
            def _(p=p):
                ring(chunk, "far", p).start()

        together(gated.at[1, 0, chunk], c_send.at[0], c_recv.at[chunk, 1]).wait_recv()
        for slot, p in ((1, 1), (3, 0)):
            pair(chunk, slot, p).start()

    def cross(chunk):
        @pl.when(second_core)
        def _():
            for slot, p in ((1, 0), (3, 1)):
                pair(chunk, slot, p).wait_recv()
                ring(chunk, "cross", p).start()

    def far(chunk):
        @pl.when(second_core)
        def _():
            together(gated.at[2, :, chunk], c_send.at[0], c_recv.at[chunk, 3]).wait_recv()
            for column in (0, 1):
                for p in (0, 1):
                    pair(chunk, 2, p, column).start()

    def arrived_pairs(chunk, slot):
        if slot == 0:
            together(gated.at[0, 1, chunk], s_send.at[0], s_recv.at[chunk, 0]).wait_recv()
        elif slot == 2:

            @pl.when(first_core)
            def _():
                together(gated.at[2, :, chunk], s_send.at[0], s_recv.at[chunk, 1]).wait_recv()

        else:
            ahead = 0 if slot == 1 else 1

            @pl.when(first_core)
            def _():
                pair(chunk, slot, ahead).wait_recv()

            pair(chunk, slot, 1 - ahead).wait_recv()

    def project(items, first=False, last=False):
        lefts, rights = [], []
        for chunk, slot in items:
            arrived_pairs(chunk, slot)
            if chunk == 0 and slot == 0:
                loads[14].wait()
            y_from = lax.rem(y_me + SIDE - slot, SIDE)
            width = LANES // 2
            for c in (core, 1 - core):
                start = pl.multiple_of((2 * y_from + c) * CH + chunk * width, width)
                rights += [v_weight[pl.ds(start, width), :]] * 2
            lefts += [gated[slot, 0, chunk], gated[slot, 1, chunk]]
        left = jnp.concatenate(lefts, axis=1)
        upper = lane_bit(left.shape, LANES // 2)
        none = jnp.zeros_like(left)
        left = jnp.concatenate([jnp.where(upper, none, left), jnp.where(upper, left, none)], axis=0)
        term = dot(left, jnp.concatenate(rights, axis=0))
        if not first:
            term = acc[...] + term
        if last:
            rows = term.astype(BF16).reshape(2, PER, PHASES // 2, FEATURES)
            for h in (0, 1):
                for r in range(PER):
                    start = r * PHASES + h * (PHASES // 2)
                    out[start : start + PHASES // 2] = rows[h, r]
        else:
            acc[...] = term

    prepare()
    for chunk in range(SUBS):
        convolve(chunk)
    for chunk in range(SUBS):
        gate(chunk)
    together(recv.at[:, pl.ds(0, CTX - 1)], a_send.at[0], s_recv.at[0, 0]).wait_send()
    near(0)
    together(y_recv.at[:, pl.ds(0, CTX - 1)], b_send.at[0], s_recv.at[0, 0]).wait_send()
    near(1)
    near(2)
    cross(0)
    project([(0, 0)], first=True)
    near(3)
    cross(1)
    project([(1, 0)])
    cross(2)
    far(0)
    project([(2, 0), (0, 1), (0, 3)])
    cross(3)
    far(1)
    project([(3, 0), (1, 1), (1, 3)])
    far(2)
    project([(0, 2), (2, 1), (2, 3)])
    far(3)
    project([(1, 2), (3, 1), (3, 3)])
    project([(2, 2), (3, 2)], last=True)

    def sent(ref, send_sem):
        together(ref, send_sem, s_recv.at[0, 0]).wait_send()

    sent(gated.at[0], c_send.at[0])
    sent(gated.at[0, 0], s_send.at[0])
    sent(gated.at[0], s_send.at[1])

    @pl.when(second_core)
    def _():
        sent(gated.at[0], c_send.at[1])
        sent(gated.at[0], s_send.at[2])


def on_device(inner_gate, outer_gate, source_values, filter_taps, skip_gain, output_weight):
    constants = [jnp.asarray(table) for table in tables()]
    operands = (inner_gate, outer_gate, source_values, filter_taps, skip_gain.reshape(1, CH), output_weight, *constants)
    vmem = pltpu.VMEM
    dma = pltpu.SemaphoreType.DMA
    return pl.pallas_call(
        kernel,
        out_shape=jax.ShapeDtypeStruct((TOK, FEATURES), BF16),
        in_specs=[pl.BlockSpec(memory_space=pltpu.HBM)] * len(operands),
        out_specs=pl.BlockSpec(memory_space=pltpu.VMEM),
        scratch_shapes=[
            vmem((TILES, TOK, LANES), BF16),
            vmem((TOK, CH), BF16),
            vmem((TILES, TOK, LANES), BF16),
            vmem((TILES, TOK, LANES), F32),
            vmem((1, CH), F32),
            vmem((output_weight.shape[0], FEATURES), BF16),
            *[vmem(table.shape, table.dtype) for table in constants],
            vmem((TILES, TOK, LANES), F32),
            vmem((SUBS, CTX, PER, 2 * LANES), BF16),
            vmem((SUBS, CTX, PER, 2 * LANES), BF16),
            vmem((SUBS, CTX, PER, LANES), BF16),
            vmem((SUBS, CTX, PER, LANES), BF16),
            vmem((HALF, LANES), F32),
            vmem((SUBS, HALF, LANES), F32),
            vmem((SUBS, HALF, LANES), F32),
            vmem((SIDE, 2, SUBS, HALF, LANES), BF16),
            vmem((TOK, FEATURES), F32),
            dma((15,)),
            dma((1,)),
            dma((SUBS,)),
            dma((1,)),
            dma((SUBS,)),
            dma((2,)),
            dma((SUBS, 4)),
            dma((3,)),
            dma((SUBS, 6)),
        ],
        compiler_params=pltpu.CompilerParams(
            collective_id=0, has_side_effects=True, vmem_limit_bytes=48 * 1024 * 1024
        ),
        cost_estimate=pl.CostEstimate(flops=3 * 10**9, bytes_accessed=8 * 10**6, transcendentals=0),
        name="hyena",
    )(*[pltpu.with_memory_space_constraint(operand, pltpu.HBM) for operand in operands])


def solution(mesh):
    in_specs = (P("ctx", "ch"), P("ctx", "ch"), P("ctx", "ch"), P("ctx", "ch"), P("ch"), P())
    out_specs = P("ctx", "ch")
    return jax.shard_map(
        on_device, mesh=mesh, in_specs=in_specs, out_specs=out_specs, check_vma=False
    )
```
